256 devices in a mesh: blk: 64 (over y, x, z_hi), rep: 4 (over z_lo, core).
Axes of the slice: x: 4, y: 4, z: 8 (z_hi: 4, z_lo: 2; z = z_hi * 2 + z_lo), core: 2. Of those that a mesh axis runs over, the one named last changes fastest.
Arguments:
- coords: float32 [3, 1200, 16384], P(None, 'rep', 'blk'), may hold values from -40 to 40
- frame_count: int32 [64], P('blk'), may hold values from 64 to 256, as said below
Outputs:
- deviation_behind: float32 [3, 16384, 256], P(None, ('blk', 'rep'))
- deviation_ahead: float32 [3, 16384, 256], P(None, ('blk', 'rep'))
The draws below stay inside these ranges and needn't reach their ends.
Inputs may be any that keep to these rules, and one draw needn't show every extreme that they name: `frame_count`: at least one block is full and at least one holds exactly 64 frames.
All inputs are finite; a program needn't handle non-finite values.
Results may differ from the reference program's by a relative error of at most 0.0003.
Values sent between devices are 32-bit elements; how exact they have to be, the bound alone decides.
No kernel may reach another device: no remote copies, remote signals or barrier semaphores. Data moves between devices by JAX's collectives and lax.ppermute only.
A program may use at most 64 MiB of HBM per device.

```python
import math
import jax
import jax.numpy as jnp
from jax import lax

FR_BLK = 256
NATOM = 1200
ROUNDS = 3
NEWTON = 4
BLOCKS = 64
FRAMES = 16384


def rotation_tables(quat):
    norm_q = jnp.sqrt(jnp.sum(quat * quat, axis=0))
    w_part = quat[0] / norm_q
    x_part = quat[1] / norm_q
    y_part = quat[2] / norm_q
    z_part = quat[3] / norm_q
    row_one = jnp.stack([1.0 - 2.0 * (y_part * y_part + z_part * z_part), 2.0 * (x_part * y_part - w_part * z_part), 2.0 * (x_part * z_part + w_part * y_part)], 0)
    row_two = jnp.stack([2.0 * (x_part * y_part + w_part * z_part), 1.0 - 2.0 * (x_part * x_part + z_part * z_part), 2.0 * (y_part * z_part - w_part * x_part)], 0)
    row_three = jnp.stack([2.0 * (x_part * z_part - w_part * y_part), 2.0 * (y_part * z_part + w_part * x_part), 1.0 - 2.0 * (x_part * x_part + y_part * y_part)], 0)
    return jnp.stack([row_one, row_two, row_three], 0)


def draw_coords(key, part):
    pieces = jax.random.split(key, 5)
    scales = jnp.array([1.5, 1.0, 0.6], jnp.float32).reshape(3, 1)
    structure = jax.random.normal(pieces[0], (3, NATOM), jnp.float32) * scales
    quat = jax.random.normal(pieces[4], (4, FRAMES), jnp.float32)
    rotation = rotation_tables(quat)
    rotated = jnp.einsum('klf,la->kaf', rotation, structure)
    amplitude = jnp.exp(jax.random.uniform(pieces[1], (1, 1, FRAMES), jnp.float32, math.log(0.7), math.log(2.5)))
    noise = jax.random.normal(pieces[2], (3, NATOM, FRAMES), jnp.float32)
    offset = 3.0 * jax.random.normal(pieces[3], (3, 1, FRAMES), jnp.float32)
    return jnp.clip(rotated + amplitude * noise + offset, -40.0, 40.0).astype(jnp.float32)


def draw_frame_count(key, part):
    first, second = jax.random.split(key)
    counts = jax.random.randint(first, (BLOCKS,), FR_BLK // 4, FR_BLK + 1, jnp.int32)
    chosen = jax.random.randint(second, (), 0, BLOCKS, jnp.int32)
    shortest = (chosen + 1) % BLOCKS
    indices = jnp.arange(BLOCKS, dtype=jnp.int32)
    counts = jnp.where(indices == shortest, FR_BLK // 4, counts)
    return jnp.where(indices == chosen, FR_BLK, counts).astype(jnp.int32)


def setup_inputs(seed: int = 0) -> dict:
    keys = jax.random.split(jax.random.key(seed), 3)
    coords = draw_coords(jax.random.fold_in(keys[2], 71), 0)
    frame_count = draw_frame_count(jax.random.fold_in(keys[2], 71), 0)
    return dict(coords=coords, frame_count=frame_count)


def pair_minor(upper, lower, left, right):
    return upper[left] * lower[right] - upper[right] * lower[left]


def deviation(covariance, own_sq, other_sq):
    m = [[covariance[first, :, second, :] for second in range(3)] for first in range(3)]
    keyed = [
        [m[0][0] + m[1][1] + m[2][2], m[1][2] - m[2][1], m[2][0] - m[0][2], m[0][1] - m[1][0]],
        [m[1][2] - m[2][1], m[0][0] - m[1][1] - m[2][2], m[0][1] + m[1][0], m[2][0] + m[0][2]],
        [m[2][0] - m[0][2], m[0][1] + m[1][0], -m[0][0] + m[1][1] - m[2][2], m[1][2] + m[2][1]],
        [m[0][1] - m[1][0], m[2][0] + m[0][2], m[1][2] + m[2][1], -m[0][0] - m[1][1] + m[2][2]],
    ]
    top_one, top_two, low_one, low_two = keyed
    det_key = (pair_minor(top_one, top_two, 0, 1) * pair_minor(low_one, low_two, 2, 3)
               - pair_minor(top_one, top_two, 0, 2) * pair_minor(low_one, low_two, 1, 3)
               + pair_minor(top_one, top_two, 0, 3) * pair_minor(low_one, low_two, 1, 2)
               + pair_minor(top_one, top_two, 1, 2) * pair_minor(low_one, low_two, 0, 3)
               - pair_minor(top_one, top_two, 1, 3) * pair_minor(low_one, low_two, 0, 2)
               + pair_minor(top_one, top_two, 2, 3) * pair_minor(low_one, low_two, 0, 1))
    det_three = (m[0][0] * (m[1][1] * m[2][2] - m[1][2] * m[2][1])
                 - m[0][1] * (m[1][0] * m[2][2] - m[1][2] * m[2][0])
                 + m[0][2] * (m[1][0] * m[2][1] - m[1][1] * m[2][0]))
    square_sum = m[0][0] * m[0][0]
    for first in range(3):
        for second in range(3):
            if first + second > 0:
                square_sum = square_sum + m[first][second] * m[first][second]
    second_coef = -2.0 * square_sum
    first_coef = -8.0 * det_three
    total = own_sq[:, None] + other_sq[None, :]
    largest = 0.5 * total
    for newton_step in range(NEWTON):
        squared = largest * largest
        polynomial = squared * squared + second_coef * squared + first_coef * largest + det_key
        derivative = 4.0 * squared * largest + 2.0 * second_coef * largest + first_coef
        largest = largest - polynomial / derivative
    return total - 2.0 * largest


def reference(coords, frame_count):
    centroid = jnp.sum(coords, axis=1, keepdims=True) / NATOM
    centered = coords - centroid
    self_sq = jnp.sum(centered * centered, axis=(0, 1)) / NATOM
    blocked = centered.reshape(3, NATOM, BLOCKS, FR_BLK)
    block_sq = self_sq.reshape(BLOCKS, FR_BLK)
    valid = jnp.arange(FR_BLK, dtype=jnp.int32)[None, :] < frame_count[:, None]
    behind_list = []
    ahead_list = []
    for distance in range(1, ROUNDS + 1):
        def one_pair(block, shift_by=distance):
            partner = ((block - shift_by) % BLOCKS).astype(jnp.int32)
            own_block = lax.dynamic_index_in_dim(blocked, block, 2, keepdims=False)
            partner_block = lax.dynamic_index_in_dim(blocked, partner, 2, keepdims=False)
            covariance = lax.dot_general(own_block, partner_block, (((1,), (1,)), ((), ())),
                                         precision=lax.Precision.HIGHEST) / NATOM
            own_sq = lax.dynamic_index_in_dim(block_sq, block, 0, keepdims=False)
            other_sq = lax.dynamic_index_in_dim(block_sq, partner, 0, keepdims=False)
            own_valid = lax.dynamic_index_in_dim(valid, block, 0, keepdims=False)
            other_valid = lax.dynamic_index_in_dim(valid, partner, 0, keepdims=False)
            mask = own_valid[:, None] & other_valid[None, :]
            return jnp.where(mask, deviation(covariance, own_sq, other_sq), 0.0)

        pair_blocks = lax.map(one_pair, jnp.arange(BLOCKS, dtype=jnp.int32))
        behind_list.append(pair_blocks.reshape(FRAMES, FR_BLK))
        rolled = jnp.roll(pair_blocks, -distance, axis=0)
        ahead_list.append(jnp.transpose(rolled, (0, 2, 1)).reshape(FRAMES, FR_BLK))
    return jnp.stack(behind_list, 0), jnp.stack(ahead_list, 0)
```

```python
import functools

import jax
import jax.numpy as jnp
from jax import lax
from jax.experimental import pallas as pl
from jax.experimental.pallas import tpu as pltpu
from jax.sharding import PartitionSpec as P

NATOM = 1200
NEWTON = 4
PIECE = 320
DEPTH = 4 * PIECE
VMEM_LIMIT = 50 * 1024 * 1024


def route(array, target):
    blocks, reps = lax.axis_size("blk"), lax.axis_size("rep")
    pairs = []
    for block in range(blocks):
        for rep in range(reps):
            to_block, to_rep = target(block, rep)
            pairs.append((block * reps + rep, (to_block % blocks) * reps + to_rep))
    return lax.ppermute(array, ("blk", "rep"), pairs)


def other_core(block, rep):
    return block, rep ^ 1


def other_chip(block, rep):
    return block, rep ^ 2


def to_neighbour(block, rep):
    return (block - 1, rep + 2) if rep < 2 else (block - 3, rep - 2)


def onward(block, rep):
    return (block + 1, rep) if rep < 2 else (block - 1, rep)


def pair_minor(upper, lower, left, right):
    return upper[left] * lower[right] - upper[right] * lower[left]


def deviation(m, total):
    keyed = [
        [m[0][0] + m[1][1] + m[2][2], m[1][2] - m[2][1], m[2][0] - m[0][2], m[0][1] - m[1][0]],
        [m[1][2] - m[2][1], m[0][0] - m[1][1] - m[2][2], m[0][1] + m[1][0], m[2][0] + m[0][2]],
        [m[2][0] - m[0][2], m[0][1] + m[1][0], -m[0][0] + m[1][1] - m[2][2], m[1][2] + m[2][1]],
        [m[0][1] - m[1][0], m[2][0] + m[0][2], m[1][2] + m[2][1], -m[0][0] - m[1][1] + m[2][2]],
    ]
    top_one, top_two, low_one, low_two = keyed
    det_key = (
        pair_minor(top_one, top_two, 0, 1) * pair_minor(low_one, low_two, 2, 3)
        - pair_minor(top_one, top_two, 0, 2) * pair_minor(low_one, low_two, 1, 3)
        + pair_minor(top_one, top_two, 0, 3) * pair_minor(low_one, low_two, 1, 2)
        + pair_minor(top_one, top_two, 1, 2) * pair_minor(low_one, low_two, 0, 3)
        - pair_minor(top_one, top_two, 1, 3) * pair_minor(low_one, low_two, 0, 2)
        + pair_minor(top_one, top_two, 2, 3) * pair_minor(low_one, low_two, 0, 1)
    )
    det_three = (
        m[0][0] * (m[1][1] * m[2][2] - m[1][2] * m[2][1])
        - m[0][1] * (m[1][0] * m[2][2] - m[1][2] * m[2][0])
        + m[0][2] * (m[1][0] * m[2][1] - m[1][1] * m[2][0])
    )
    square_sum = m[0][0] * m[0][0]
    for first in range(3):
        for second in range(3):
            if first + second > 0:
                square_sum = square_sum + m[first][second] * m[first][second]
    second_coef = -2.0 * square_sum
    first_coef = -8.0 * det_three
    largest = 0.5 * total
    for _ in range(NEWTON):
        squared = largest * largest
        polynomial = squared * squared + second_coef * squared + first_coef * largest + det_key
        derivative = 4.0 * squared * largest + 2.0 * second_coef * largest + first_coef
        largest = largest - polynomial / derivative
    return total - 2.0 * largest


def padded(value):
    return jnp.concatenate([value, jnp.zeros((PIECE - value.shape[0], value.shape[1]), value.dtype)], 0)


def halves(value):
    high = value.astype(jnp.bfloat16)
    return high, (value - high.astype(jnp.float32)).astype(jnp.bfloat16)


def prepare_kernel(a_ref, b_ref, c_ref, d_ref, high_ref, low_ref, square_ref):
    frames = a_ref.shape[2]
    square = jnp.zeros((1, frames), jnp.float32)
    for comp in range(3):
        pieces = [ref[comp] for ref in (a_ref, b_ref, c_ref, d_ref)]
        centroid = sum(jnp.sum(piece, axis=0, keepdims=True) for piece in pieces) / NATOM
        for place, piece in enumerate(pieces):
            centered = piece - centroid
            square = square + jnp.sum(centered * centered, axis=0, keepdims=True)
            high, low = halves(padded(centered))
            high_ref[place * PIECE:(place + 1) * PIECE, comp * frames:(comp + 1) * frames] = high
            low_ref[place * PIECE:(place + 1) * PIECE, comp * frames:(comp + 1) * frames] = low
    square_ref[...] = jnp.broadcast_to(square / NATOM, square_ref.shape)


def covariance(refs, lane, row, rows, high_ref, low_ref, turned, left_high, left_low, acc, other_sq):
    square = jnp.zeros((turned.shape[0], 1), jnp.float32)
    for comp in range(3):
        pieces = [ref[comp, :, pl.ds(lane, 128)] for ref in refs]
        centroid = sum(jnp.sum(piece, axis=0, keepdims=True) for piece in pieces) / NATOM
        stacked = jnp.concatenate([padded(piece - centroid) for piece in pieces], 0)
        turned[...] = stacked.T
        used = turned[pl.ds(row, rows), :]
        square = jnp.sum(used * used, axis=1, keepdims=True) + (square if comp else 0.0)
        high, low = halves(used)
        left_high[comp * rows:(comp + 1) * rows, :] = high
        left_low[comp * rows:(comp + 1) * rows, :] = low
    dot = functools.partial(jnp.dot, preferred_element_type=jnp.float32)
    acc[...] = (
        dot(left_high[...], high_ref[...])
        + dot(left_high[...], low_ref[...])
        + dot(left_low[...], high_ref[...])
    )
    other_sq[...] = jnp.broadcast_to(square / NATOM, other_sq.shape)


def fill_tile(acc, rows, first_row, other_count, own_count, own_sq, other_sq, tile):
    frames = own_sq.shape[1]
    own_valid = lax.broadcasted_iota(jnp.int32, (8, frames), 1) < own_count
    place = lax.broadcasted_iota(jnp.int32, (8, frames), 0)
    for at in range(0, rows, 8):
        m = [
            [acc[i * rows + at:i * rows + at + 8, j * frames:(j + 1) * frames] * (1.0 / NATOM) for j in range(3)]
            for i in range(3)
        ]
        total = own_sq[...] + other_sq[at:at + 8, 0:1]
        valid = own_valid & (place + (first_row + at) < other_count)
        tile[at:at + 8, :] = jnp.where(valid, deviation(m, total), 0.0)


def near_kernel(info, high_ref, low_ref, own_sq, a, b, c, d, out_a, out_b, tile, turned, left_high, left_low, acc, other_sq):
    low_place, core, own_count, count = info[0], info[1], info[2], info[3]
    lane = pl.multiple_of(core * 128, 128)
    covariance((a, b, c, d), lane, 0, 128, high_ref, low_ref, turned, left_high, left_low, acc, other_sq)
    fill_tile(acc, 128, core * 128, count, own_count, own_sq, other_sq, tile)
    out_a[...] = tile[pl.ds(pl.multiple_of((1 - low_place) * 64, 64), 64), :]
    out_b[...] = tile[pl.ds(pl.multiple_of(low_place * 64, 64), 64), :]


def far_kernel(info, high_ref, low_ref, own_sq, a, b, c, d, near, tile, parts, turned, left_high, left_low, acc, other_sq):
    low_place, core, own_count, count = info[0], info[1], info[2], info[4]
    row = pl.multiple_of(core * 64, 64)
    covariance((a, b, c, d), 0, row, 64, high_ref, low_ref, turned, left_high, left_low, acc, other_sq)
    fill_tile(acc, 64, low_place * 128 + core * 64, count, own_count, own_sq, other_sq, tile)
    parts[:, :, 0:128] = near[...].T.reshape(4, 64, 128)
    parts[:, :, 128:192] = tile[...].T.reshape(4, 64, 64)
    parts[:, :, 192:256] = jnp.zeros((4, 64, 64), jnp.float32)


def finish_kernel(info, got_a, got_b, got_far, parts, behind, ahead):
    odd = info[1] == 1
    one, two = got_a[...], got_b[...]
    behind[0] = jnp.where(odd, two, one)
    behind[1] = got_far[...]
    behind[2] = jnp.where(odd, one, two)
    ahead[0] = jnp.concatenate([parts[2, :, 0:128], parts[3, :, 0:128]], 1)
    ahead[1] = jnp.concatenate([parts[i, :, 128:192] for i in range(4)], 1)
    ahead[2] = jnp.concatenate([parts[0, :, 0:128], parts[1, :, 0:128]], 1)


def call(kernel, out_shapes, scratch=()):
    def run(*args):
        whole = pl.BlockSpec(memory_space=pltpu.VMEM)
        specs = [pl.BlockSpec(memory_space=pltpu.SMEM) if arg.dtype == jnp.int32 else whole for arg in args]
        return pl.pallas_call(
            kernel,
            out_shape=out_shapes,
            in_specs=specs,
            out_specs=jax.tree.map(lambda _: whole, out_shapes),
            scratch_shapes=list(scratch),
            compiler_params=pltpu.CompilerParams(vmem_limit_bytes=VMEM_LIMIT),
        )(*args)

    return run


def f32(*shape):
    return jax.ShapeDtypeStruct(shape, jnp.float32)


def scratch_of(used, frames):
    return (
        pltpu.VMEM((128, DEPTH), jnp.float32),
        pltpu.VMEM((3 * used, DEPTH), jnp.bfloat16),
        pltpu.VMEM((3 * used, DEPTH), jnp.bfloat16),
        pltpu.VMEM((3 * used, 3 * frames), jnp.float32),
        pltpu.VMEM((used, 128), jnp.float32),
    )


def shards(coords, frame_count):
    frames = coords.shape[2]
    rep = lax.axis_index("rep")
    low_place, core = rep // 2, rep % 2
    near_count = route(frame_count, to_neighbour)
    far_count = route(frame_count, lambda block, rep: (block - 2, rep))

    own_chip = route(coords, other_chip)
    near_a = route(coords, to_neighbour)
    own_core = route(coords, other_core)
    near_b = route(own_chip, to_neighbour)
    far_a = route(lax.dynamic_slice_in_dim(near_a, low_place * 128, 128, 2), onward)
    own_both = route(own_chip, other_core)
    near_a_core = route(near_a, other_core)
    far_b = route(lax.dynamic_slice_in_dim(near_b, low_place * 128, 128, 2), onward)
    near_b_core = route(near_b, other_core)
    far_a_core = route(far_a, other_core)
    far_b_core = route(far_b, other_core)

    info = jnp.concatenate([low_place[None], core[None], frame_count, near_count, far_count]).astype(jnp.int32)
    wide = jax.ShapeDtypeStruct((DEPTH, 3 * frames), jnp.bfloat16)
    high, low, own_sq = call(prepare_kernel, (wide, wide, f32(8, frames)))(coords, own_chip, own_core, own_both)
    near_out_a, near_out_b, near_tile = call(
        near_kernel, (f32(64, frames), f32(64, frames), f32(128, frames)), scratch_of(128, frames)
    )(info, high, low, own_sq, near_b, near_a, near_b_core, near_a_core)
    got_a = route(near_out_a, lambda b, r: (b + 1, 2 * (r % 2)) if r >= 2 else (b + 3, 2 * (r % 2) + 1))
    got_b = route(near_out_b, lambda b, r: (b + 1, 2 * (r % 2) + 1) if r >= 2 else (b + 3, 2 * (r % 2)))
    far_tile, parts = call(far_kernel, (f32(64, frames), f32(4, 64, frames)), scratch_of(64, frames))(
        info, high, low, own_sq, far_b, far_a, far_b_core, far_a_core, near_tile
    )
    got_far = route(far_tile, lambda block, rep: (block + 2, 2 * (rep // 2) + rep % 2))
    parts = lax.all_to_all(parts, "rep", 0, 0)
    return call(finish_kernel, (f32(3, 64, frames), f32(3, 64, frames)))(info, got_a, got_b, got_far, parts)


def solution(mesh):
    in_specs = (P(None, "rep", "blk"), P("blk"))
    out_specs = (P(None, ("blk", "rep"), None), P(None, ("blk", "rep"), None))
    return jax.shard_map(shards, mesh=mesh, in_specs=in_specs, out_specs=out_specs, check_vma=False)
```

```python
import functools

import jax
import jax.numpy as jnp
from jax import lax
from jax.experimental import pallas as pl
from jax.experimental.pallas import tpu as pltpu
from jax.sharding import PartitionSpec as P

NATOM = 1200
NEWTON = 4
PIECE = 320
DEPTH = 4 * PIECE
VMEM_LIMIT = 12 * 1024 * 1024


def route(array, target):
    blocks, reps = lax.axis_size("blk"), lax.axis_size("rep")
    pairs = []
    for block in range(blocks):
        for rep in range(reps):
            to_block, to_rep = target(block, rep)
            pairs.append((block * reps + rep, (to_block % blocks) * reps + to_rep))
    return lax.ppermute(array, ("blk", "rep"), pairs)


def other_core(block, rep):
    return block, rep ^ 1


def other_chip(block, rep):
    return block, rep ^ 2


def to_neighbour(block, rep):
    return (block - 1, rep + 2) if rep < 2 else (block - 3, rep - 2)


def pair_minor(upper, lower, left, right):
    return upper[left] * lower[right] - upper[right] * lower[left]


def deviation(m, total):
    keyed = [
        [m[0][0] + m[1][1] + m[2][2], m[1][2] - m[2][1], m[2][0] - m[0][2], m[0][1] - m[1][0]],
        [m[1][2] - m[2][1], m[0][0] - m[1][1] - m[2][2], m[0][1] + m[1][0], m[2][0] + m[0][2]],
        [m[2][0] - m[0][2], m[0][1] + m[1][0], -m[0][0] + m[1][1] - m[2][2], m[1][2] + m[2][1]],
        [m[0][1] - m[1][0], m[2][0] + m[0][2], m[1][2] + m[2][1], -m[0][0] - m[1][1] + m[2][2]],
    ]
    top_one, top_two, low_one, low_two = keyed
    det_key = (
        pair_minor(top_one, top_two, 0, 1) * pair_minor(low_one, low_two, 2, 3)
        - pair_minor(top_one, top_two, 0, 2) * pair_minor(low_one, low_two, 1, 3)
        + pair_minor(top_one, top_two, 0, 3) * pair_minor(low_one, low_two, 1, 2)
        + pair_minor(top_one, top_two, 1, 2) * pair_minor(low_one, low_two, 0, 3)
        - pair_minor(top_one, top_two, 1, 3) * pair_minor(low_one, low_two, 0, 2)
        + pair_minor(top_one, top_two, 2, 3) * pair_minor(low_one, low_two, 0, 1)
    )
    det_three = (
        m[0][0] * (m[1][1] * m[2][2] - m[1][2] * m[2][1])
        - m[0][1] * (m[1][0] * m[2][2] - m[1][2] * m[2][0])
        + m[0][2] * (m[1][0] * m[2][1] - m[1][1] * m[2][0])
    )
    square_sum = m[0][0] * m[0][0]
    for first in range(3):
        for second in range(3):
            if first + second > 0:
                square_sum = square_sum + m[first][second] * m[first][second]
    second_coef = -2.0 * square_sum
    first_coef = -8.0 * det_three
    largest = 0.5 * total
    for _ in range(NEWTON):
        squared = largest * largest
        polynomial = squared * squared + second_coef * squared + first_coef * largest + det_key
        derivative = 4.0 * squared * largest + 2.0 * second_coef * largest + first_coef
        largest = largest - polynomial / derivative
    return total - 2.0 * largest


def padded(value):
    return jnp.concatenate([value, jnp.zeros((PIECE - value.shape[0], value.shape[1]), value.dtype)], 0)


def halves(value):
    high = value.astype(jnp.bfloat16)
    return high, (value - high.astype(jnp.float32)).astype(jnp.bfloat16)


def place_of():
    rep = lax.axis_index("rep")
    return rep // 2, rep % 2


def aligned(index, size):
    return pl.ds(pl.multiple_of(index * size, size), size)


def column_sums(pieces):
    return sum(jnp.sum(piece, axis=0, keepdims=True) for piece in pieces)


def products(left_high, left_low, right_high, right_low):
    dot = functools.partial(jnp.dot, preferred_element_type=jnp.float32)
    return dot(left_high, right_high) + dot(left_high, right_low) + dot(left_low, right_high)


def prepare_kernel(a_ref, b_ref, c_ref, d_ref, high_ref, low_ref, square_ref):
    frames = a_ref.shape[2]
    square = jnp.zeros((frames, 1), jnp.float32)
    for comp in range(3):
        pieces = [ref[comp] for ref in (a_ref, b_ref, c_ref, d_ref)]
        centroid = column_sums(pieces) / NATOM
        value = jnp.concatenate([padded(piece - centroid) for piece in pieces], 0).T
        square = square + jnp.sum(value * value, axis=1, keepdims=True)
        high, low = halves(value)
        high_ref[comp * frames:(comp + 1) * frames, :] = high
        low_ref[comp * frames:(comp + 1) * frames, :] = low
    square_ref[...] = jnp.broadcast_to(square / NATOM, square_ref.shape)


def fill_tile(covariance, rows, row_square, column_square, row_limit, column_limit, tile):
    step = 16
    column_valid = lax.broadcasted_iota(jnp.int32, (step, 128), 1) < column_limit
    for at in range(0, rows, step):
        place = lax.broadcasted_iota(jnp.int32, (step, 128), 0) + at
        total = row_square[at:at + step, :] + column_square
        tile[at:at + step, :] = jnp.where(
            (place < row_limit) & column_valid, deviation(covariance(at, at + step), total), 0.0
        )


def right_side(refs, lanes, about, right_high, right_low):
    total, square = [], jnp.zeros((1, 128), jnp.float32)
    for comp in range(3):
        moved = [ref[comp, :, lanes] - about[comp:comp + 1, :] for ref in refs]
        total.append(column_sums(moved))
        square = square + column_sums([value * value for value in moved])
        for place, value in enumerate(moved):
            top, rest = halves(padded(value))
            right_high[place * PIECE:(place + 1) * PIECE, comp * 128:(comp + 1) * 128] = top
            right_low[place * PIECE:(place + 1) * PIECE, comp * 128:(comp + 1) * 128] = rest
    return total, square


def half_facts(refs, out):
    square = 0.0
    for comp in range(3):
        pieces = [ref[comp] for ref in refs]
        mean = column_sums(pieces) / (NATOM / 2)
        square = square + column_sums([(piece - mean) * (piece - mean) for piece in pieces])
        out[comp:comp + 1, :] = mean
    out[3:4, :] = square
    out[4:8, :] = jnp.zeros((4, out.shape[1]), jnp.float32)


def near_first_kernel(high, low, a, b, acc, facts, right_high, right_low):
    half_facts((a, b), facts)
    lanes = aligned(place_of()[1], 128)
    right_side((a, b), lanes, facts[:, lanes], right_high, right_low)
    acc[...] = products(high[:, DEPTH // 2:], low[:, DEPTH // 2:], right_high[...], right_low[...])


def near_kernel(own_count, count, high, low, square, first, facts, a, b, out_a, out_b, parts, right_high, right_low, acc, tile, turned):
    low_place, core = place_of()
    lanes = aligned(core, 128)
    about = facts[:, lanes]
    total, column_square = right_side((a, b), lanes, about, right_high, right_low)
    column_square = (column_square + about[3:4, :]) / NATOM
    for comp in range(3):
        offset = total[comp] / NATOM
        column_square = column_square - offset * offset
    acc[...] = first[...] + products(high[:, :DEPTH // 2], low[:, :DEPTH // 2], right_high[...], right_low[...])
    frames = square.shape[0]

    def covariance(start, stop):
        return [
            [acc[i * frames + start:i * frames + stop, j * 128:(j + 1) * 128] * (1.0 / NATOM) for j in range(3)]
            for i in range(3)
        ]

    fill_tile(covariance, frames, square, column_square, own_count[0], count[0] - core * 128, tile)
    parts[...] = tile[...].reshape(parts.shape)
    turned[...] = tile[...].T
    out_a[...] = turned[aligned(1 - low_place, 64), :]
    out_b[...] = turned[aligned(low_place, 64), :]


def between_kernel(facts, near_a, near_b, else_a, else_b, mine, give, left_high, left_low, right_high, right_low, acc, here, known):
    low_place, core = place_of()
    half_facts((near_a, near_b), here)
    sign = jnp.where(low_place == 0, 1.0, -1.0)
    square = here[3:4, :] + facts[3:4, :]
    known[...] = jnp.zeros_like(known)
    for comp in range(3):
        apart = here[comp:comp + 1, :] - facts[comp:comp + 1, :]
        known[comp:comp + 1, :] = sign * apart
        square = square + (NATOM / 4) * apart * apart
    known[3:4, :] = square / NATOM
    upper = low_place == 1
    lanes = aligned(core, 128)
    for comp in range(3):
        pieces = [
            jnp.where(upper, one[comp, :, lanes], two[comp, :, lanes]) for one, two in ((near_a, else_a), (near_b, else_b))
        ]
        mean = column_sums(pieces) / (NATOM / 2)
        value = jnp.concatenate([padded(piece - mean) for piece in pieces], 0).T
        high, low = halves(value)
        left_high[comp * 128:(comp + 1) * 128, :] = high
        left_low[comp * 128:(comp + 1) * 128, :] = low
        pieces = [jnp.where(upper, two[comp], one[comp]) for one, two in ((near_a, else_a), (near_b, else_b))]
        mean = column_sums(pieces) / (NATOM / 2)
        for place, piece in enumerate(pieces):
            high, low = halves(padded(piece - mean))
            right_high[place * PIECE:(place + 1) * PIECE, comp * 256:(comp + 1) * 256] = high
            right_low[place * PIECE:(place + 1) * PIECE, comp * 256:(comp + 1) * 256] = low
    acc[...] = products(left_high[...], left_low[...], right_high[...], right_low[...])
    for i in range(3):
        for j in range(3):
            to = pl.ds((3 * i + j) * 128, 128)
            mine[to, :] = acc[i * 128:(i + 1) * 128, aligned(2 * j + low_place, 128)]
            give[to, :] = acc[i * 128:(i + 1) * 128, aligned(2 * j + 1 - low_place, 128)]
    mine[1152:1160, :] = known[:, aligned(jnp.where(upper, core, 0), 128)]
    give[1152:1160, :] = known[:, aligned(jnp.where(upper, core, 1), 128)]


def far_kernel(count_one, count_three, mine, got, ahead_a, ahead_b, behind_a, behind_b, tile, square):
    low_place, core = place_of()
    one, two = mine[1152:1160, :], got[1152:1160, :]
    row_facts = jnp.where(low_place == 1, one, two).T
    column_facts = jnp.where(low_place == 1, two, one)
    square[...] = jnp.broadcast_to(row_facts[:, 3:4], square.shape)

    def covariance(start, stop):
        return [
            [
                (mine[(3 * i + j) * 128 + start:(3 * i + j) * 128 + stop, :]
                 + got[(3 * i + j) * 128 + start:(3 * i + j) * 128 + stop, :]) * (1.0 / NATOM)
                + (0.25 * row_facts[start:stop, i:i + 1]) * column_facts[j:j + 1, :]
                for j in range(3)
            ]
            for i in range(3)
        ]

    fill_tile(
        covariance, 128, square, column_facts[3:4, :], count_one[0] - core * 128, count_three[0] - low_place * 128, tile
    )
    ahead_a[...] = tile[aligned(low_place, 64), :]
    ahead_b[...] = tile[aligned(1 - low_place, 64), :]
    tile[...] = tile[...].T
    behind_a[...] = tile[aligned(core, 64), :]
    behind_b[...] = tile[aligned(1 - core, 64), :]


def finish_kernel(got_a, got_b, parts, ahead_a, ahead_b, behind_a, behind_b, behind, ahead):
    core = place_of()[1]

    def ordered(one, two):
        return jnp.where(core == 1, two, one), jnp.where(core == 1, one, two)

    behind[0], behind[2] = ordered(got_a[...], got_b[...])
    behind[1] = jnp.concatenate(ordered(behind_a[...], behind_b[...]), 1)
    ahead[0] = jnp.concatenate([parts[2], parts[3]], 1)
    ahead[1] = jnp.concatenate(ordered(ahead_a[...], ahead_b[...]), 1)
    ahead[2] = jnp.concatenate([parts[0], parts[1]], 1)


def call(kernel, out_shapes, microseconds, scratch=()):
    def run(*args):
        whole = pl.BlockSpec(memory_space=pltpu.VMEM)
        specs = [pl.BlockSpec(memory_space=pltpu.SMEM) if arg.dtype == jnp.int32 else whole for arg in args]
        return pl.pallas_call(
            kernel,
            out_shape=out_shapes,
            in_specs=specs,
            out_specs=jax.tree.map(lambda _: whole, out_shapes),
            scratch_shapes=[pltpu.VMEM(shape, dtype) for shape, dtype in scratch],
            cost_estimate=pl.CostEstimate(flops=0, bytes_accessed=int(microseconds * 3.6e6), transcendentals=0),
            compiler_params=pltpu.CompilerParams(vmem_limit_bytes=VMEM_LIMIT),
        )(*args)

    return run


def f32(*shape):
    return jax.ShapeDtypeStruct(shape, jnp.float32)


def bf16(*shape):
    return jax.ShapeDtypeStruct(shape, jnp.bfloat16)


def shards(coords, frame_count):
    frames = coords.shape[2]
    together = lax.optimization_barrier
    small, wide = jnp.bfloat16, jnp.float32

    own_chip = route(coords, other_chip)
    near_a = route(coords, to_neighbour)
    own_core = route(coords, other_core)
    count_one = route(frame_count, lambda block, rep: (block - 1, rep))
    count_three = route(frame_count, lambda block, rep: (block - 3, rep))
    own_chip, near_a = together((own_chip, near_a))

    near_b = route(own_chip, to_neighbour)
    else_a = route(near_a, other_chip)
    own_both = route(own_chip, other_core)
    near_a_core = route(near_a, other_core)
    high, low, square = call(
        prepare_kernel, (bf16(768, DEPTH), bf16(768, DEPTH), f32(frames, 128)), 4.0
    )(coords, own_core, own_chip, own_both)
    sides = [((DEPTH // 2, 384), small), ((DEPTH // 2, 384), small)]
    near_first, facts = call(near_first_kernel, (f32(768, 384), f32(8, 256)), 4.0, sides)(high, low, near_a, near_a_core)
    near_b, else_a, near_first, facts, count_one, count_three = together(
        (near_b, else_a, near_first, facts, count_one, count_three)
    )

    near_b_core = route(near_b, other_core)
    else_a_core = route(else_a, other_core)
    mine, give = call(
        between_kernel,
        (f32(1160, 128), f32(1160, 128)),
        3.0,
        [((384, DEPTH // 2), small), ((384, DEPTH // 2), small), ((DEPTH // 2, 768), small), ((DEPTH // 2, 768), small),
         ((384, 768), wide), ((8, 256), wide), ((8, 256), wide)],
    )(facts, near_b, near_b_core, else_a, else_a_core)
    got = route(give, other_chip)
    near_first, mine = together((near_first, mine))
    near_count = jnp.where(lax.axis_index("rep") < 2, count_three, count_one)
    near_out_a, near_out_b, parts = call(
        near_kernel,
        (f32(64, frames), f32(64, frames), f32(4, 64, 128)),
        4.0,
        sides + [((768, 384), wide), ((frames, 128), wide), ((128, frames), wide)],
    )(frame_count, near_count, high, low, square, near_first, facts, near_b, near_b_core)
    got_a = route(near_out_a, lambda b, r: (b + 1, 2 * (r % 2)) if r >= 2 else (b + 3, 2 * (r % 2) + 1))
    got_b = route(near_out_b, lambda b, r: (b + 1, 2 * (r % 2) + 1) if r >= 2 else (b + 3, 2 * (r % 2)))
    parts = lax.all_to_all(parts, "rep", 0, 0)
    got, got_a, got_b, parts = together((got, got_a, got_b, parts))

    ahead_a, ahead_b, behind_a, behind_b = call(
        far_kernel,
        (f32(64, 128), f32(64, 128), f32(64, 128), f32(64, 128)),
        1.5,
        [((128, 128), wide), ((128, 128), wide)],
    )(count_one, count_three, mine, got)
    ahead_a = route(ahead_a, lambda block, rep: (block + 1, 2 * (rep % 2) + rep // 2))
    ahead_b = route(ahead_b, lambda block, rep: (block + 1, 2 * (rep % 2) + 1 - rep // 2))
    behind_a = route(behind_a, lambda block, rep: (block + 3, rep))
    behind_b = route(behind_b, lambda block, rep: (block + 3, rep ^ 1))
    return call(finish_kernel, (f32(3, 64, frames), f32(3, 64, frames)), 1.3)(
        got_a, got_b, parts, ahead_a, ahead_b, behind_a, behind_b
    )


def solution(mesh):
    in_specs = (P(None, "rep", "blk"), P("blk"))
    out_specs = (P(None, ("blk", "rep"), None), P(None, ("blk", "rep"), None))
    return jax.shard_map(shards, mesh=mesh, in_specs=in_specs, out_specs=out_specs, check_vma=False)
```

```python
import functools

import jax
import jax.numpy as jnp
from jax import lax
from jax.experimental import pallas as pl
from jax.experimental.pallas import tpu as pltpu
from jax.sharding import PartitionSpec as P

NATOM = 1200
NEWTON = 4
PIECE = 320
DEPTH = 4 * PIECE
VMEM_LIMIT = 12 * 1024 * 1024


def route(array, target):
    blocks, reps = lax.axis_size("blk"), lax.axis_size("rep")
    pairs = []
    for block in range(blocks):
        for rep in range(reps):
            to_block, to_rep = target(block, rep)
            pairs.append((block * reps + rep, (to_block % blocks) * reps + to_rep))
    return lax.ppermute(array, ("blk", "rep"), pairs)


def other_core(block, rep):
    return block, rep ^ 1


def other_chip(block, rep):
    return block, rep ^ 2


def to_neighbour(block, rep):
    return (block - 1, rep + 2) if rep < 2 else (block - 3, rep - 2)


def pair_minor(upper, lower, left, right):
    return upper[left] * lower[right] - upper[right] * lower[left]


def deviation(m, total):
    keyed = [
        [m[0][0] + m[1][1] + m[2][2], m[1][2] - m[2][1], m[2][0] - m[0][2], m[0][1] - m[1][0]],
        [m[1][2] - m[2][1], m[0][0] - m[1][1] - m[2][2], m[0][1] + m[1][0], m[2][0] + m[0][2]],
        [m[2][0] - m[0][2], m[0][1] + m[1][0], -m[0][0] + m[1][1] - m[2][2], m[1][2] + m[2][1]],
        [m[0][1] - m[1][0], m[2][0] + m[0][2], m[1][2] + m[2][1], -m[0][0] - m[1][1] + m[2][2]],
    ]
    top_one, top_two, low_one, low_two = keyed
    det_key = (
        pair_minor(top_one, top_two, 0, 1) * pair_minor(low_one, low_two, 2, 3)
        - pair_minor(top_one, top_two, 0, 2) * pair_minor(low_one, low_two, 1, 3)
        + pair_minor(top_one, top_two, 0, 3) * pair_minor(low_one, low_two, 1, 2)
        + pair_minor(top_one, top_two, 1, 2) * pair_minor(low_one, low_two, 0, 3)
        - pair_minor(top_one, top_two, 1, 3) * pair_minor(low_one, low_two, 0, 2)
        + pair_minor(top_one, top_two, 2, 3) * pair_minor(low_one, low_two, 0, 1)
    )
    det_three = (
        m[0][0] * (m[1][1] * m[2][2] - m[1][2] * m[2][1])
        - m[0][1] * (m[1][0] * m[2][2] - m[1][2] * m[2][0])
        + m[0][2] * (m[1][0] * m[2][1] - m[1][1] * m[2][0])
    )
    square_sum = m[0][0] * m[0][0]
    for first in range(3):
        for second in range(3):
            if first + second > 0:
                square_sum = square_sum + m[first][second] * m[first][second]
    second_coef = -2.0 * square_sum
    first_coef = -8.0 * det_three
    largest = 0.5 * total
    for _ in range(NEWTON):
        squared = largest * largest
        polynomial = squared * squared + second_coef * squared + first_coef * largest + det_key
        derivative = 4.0 * squared * largest + 2.0 * second_coef * largest + first_coef
        largest = largest - polynomial / derivative
    return total - 2.0 * largest


def padded(value):
    return jnp.concatenate([value, jnp.zeros((PIECE - value.shape[0], value.shape[1]), value.dtype)], 0)


def halves(value):
    high = value.astype(jnp.bfloat16)
    return high, (value - high.astype(jnp.float32)).astype(jnp.bfloat16)


def place_of():
    rep = lax.axis_index("rep")
    return rep // 2, rep % 2


def aligned(index, size):
    return pl.ds(pl.multiple_of(index * size, size), size)


def column_sums(pieces):
    return sum(jnp.sum(piece, axis=0, keepdims=True) for piece in pieces)


def products(left_high, left_low, right_high, right_low):
    dot = functools.partial(jnp.dot, preferred_element_type=jnp.float32)
    return dot(left_high, right_high) + dot(left_high, right_low) + dot(left_low, right_high)


def prepare_kernel(a_ref, b_ref, c_ref, d_ref, high_ref, low_ref, square_ref):
    frames = a_ref.shape[2]
    square = jnp.zeros((frames, 1), jnp.float32)
    for comp in range(3):
        pieces = [ref[comp] for ref in (a_ref, b_ref, c_ref, d_ref)]
        centroid = column_sums(pieces) / NATOM
        value = jnp.concatenate([padded(piece - centroid) for piece in pieces], 0).T
        square = square + jnp.sum(value * value, axis=1, keepdims=True)
        high, low = halves(value)
        high_ref[comp * frames:(comp + 1) * frames, :] = high
        low_ref[comp * frames:(comp + 1) * frames, :] = low
    square_ref[...] = jnp.broadcast_to(square / NATOM, square_ref.shape)


def fill_tile(covariance, rows, row_square, column_square, row_limit, column_limit, tile):
    step = 16
    column_valid = lax.broadcasted_iota(jnp.int32, (step, 128), 1) < column_limit
    for at in range(0, rows, step):
        place = lax.broadcasted_iota(jnp.int32, (step, 128), 0) + at
        total = row_square[at:at + step, :] + column_square
        tile[at:at + step, :] = jnp.where(
            (place < row_limit) & column_valid, deviation(covariance(at, at + step), total), 0.0
        )


def right_side(refs, lanes, about, right_high, right_low):
    total, square = [], jnp.zeros((1, 128), jnp.float32)
    for comp in range(3):
        moved = [ref[comp, :, lanes] - about[comp:comp + 1, :] for ref in refs]
        total.append(column_sums(moved))
        square = square + column_sums([value * value for value in moved])
        for place, value in enumerate(moved):
            top, rest = halves(padded(value))
            right_high[place * PIECE:(place + 1) * PIECE, comp * 128:(comp + 1) * 128] = top
            right_low[place * PIECE:(place + 1) * PIECE, comp * 128:(comp + 1) * 128] = rest
    return total, square


def half_facts(refs, out):
    square = 0.0
    for comp in range(3):
        pieces = [ref[comp] for ref in refs]
        mean = column_sums(pieces) / (NATOM / 2)
        square = square + column_sums([(piece - mean) * (piece - mean) for piece in pieces])
        out[comp:comp + 1, :] = mean
    out[3:4, :] = square
    out[4:8, :] = jnp.zeros((4, out.shape[1]), jnp.float32)


def near_first_kernel(high, low, a, b, acc, facts, right_high, right_low):
    half_facts((a, b), facts)
    lanes = aligned(place_of()[1], 128)
    right_side((a, b), lanes, facts[:, lanes], right_high, right_low)
    acc[...] = products(high[:, DEPTH // 2:], low[:, DEPTH // 2:], right_high[...], right_low[...])


def near_kernel(own_count, count_one, count_three, high, low, square, first, facts, a, b, out_a, out_b, parts, right_high, right_low, acc, tile, turned):
    low_place, core = place_of()
    count = jnp.where(low_place == 1, count_one[0], count_three[0])
    lanes = aligned(core, 128)
    about = facts[:, lanes]
    total, column_square = right_side((a, b), lanes, about, right_high, right_low)
    column_square = (column_square + about[3:4, :]) / NATOM
    for comp in range(3):
        offset = total[comp] / NATOM
        column_square = column_square - offset * offset
    acc[...] = first[...] + products(high[:, :DEPTH // 2], low[:, :DEPTH // 2], right_high[...], right_low[...])
    frames = square.shape[0]

    def covariance(start, stop):
        return [
            [acc[i * frames + start:i * frames + stop, j * 128:(j + 1) * 128] * (1.0 / NATOM) for j in range(3)]
            for i in range(3)
        ]

    fill_tile(covariance, frames, square, column_square, own_count[0], count - core * 128, tile)
    parts[...] = tile[...].reshape(parts.shape)
    turned[...] = tile[...].T
    out_a[...] = turned[aligned(1 - low_place, 64), :]
    out_b[...] = turned[aligned(low_place, 64), :]


def between_kernel(facts, near_a, near_b, else_a, else_b, mine, give, left_high, left_low, right_high, right_low, acc, here, known):
    low_place, core = place_of()
    half_facts((near_a, near_b), here)
    sign = jnp.where(low_place == 0, 1.0, -1.0)
    square = here[3:4, :] + facts[3:4, :]
    known[...] = jnp.zeros_like(known)
    for comp in range(3):
        apart = here[comp:comp + 1, :] - facts[comp:comp + 1, :]
        known[comp:comp + 1, :] = sign * apart
        square = square + (NATOM / 4) * apart * apart
    known[3:4, :] = square / NATOM
    upper = low_place == 1
    lanes = aligned(core, 128)
    for comp in range(3):
        pieces = [
            jnp.where(upper, one[comp, :, lanes], two[comp, :, lanes]) for one, two in ((near_a, else_a), (near_b, else_b))
        ]
        mean = column_sums(pieces) / (NATOM / 2)
        value = jnp.concatenate([padded(piece - mean) for piece in pieces], 0).T
        high, low = halves(value)
        left_high[comp * 128:(comp + 1) * 128, :] = high
        left_low[comp * 128:(comp + 1) * 128, :] = low
        pieces = [jnp.where(upper, two[comp], one[comp]) for one, two in ((near_a, else_a), (near_b, else_b))]
        mean = column_sums(pieces) / (NATOM / 2)
        for place, piece in enumerate(pieces):
            high, low = halves(padded(piece - mean))
            right_high[place * PIECE:(place + 1) * PIECE, comp * 256:(comp + 1) * 256] = high
            right_low[place * PIECE:(place + 1) * PIECE, comp * 256:(comp + 1) * 256] = low
    acc[...] = products(left_high[...], left_low[...], right_high[...], right_low[...])
    for i in range(3):
        for j in range(3):
            to = pl.ds((3 * i + j) * 128, 128)
            mine[to, :] = acc[i * 128:(i + 1) * 128, aligned(2 * j + low_place, 128)]
            give[to, :] = acc[i * 128:(i + 1) * 128, aligned(2 * j + 1 - low_place, 128)]
    mine[1152:1160, :] = known[:, aligned(jnp.where(upper, core, 0), 128)]
    give[1152:1160, :] = known[:, aligned(jnp.where(upper, core, 1), 128)]


def far_kernel(count_one, count_three, mine, got, ahead_a, ahead_b, behind_a, behind_b, tile, square):
    low_place, core = place_of()
    one, two = mine[1152:1160, :], got[1152:1160, :]
    row_facts = jnp.where(low_place == 1, one, two).T
    column_facts = jnp.where(low_place == 1, two, one)
    square[...] = jnp.broadcast_to(row_facts[:, 3:4], square.shape)

    def covariance(start, stop):
        return [
            [
                (mine[(3 * i + j) * 128 + start:(3 * i + j) * 128 + stop, :]
                 + got[(3 * i + j) * 128 + start:(3 * i + j) * 128 + stop, :]) * (1.0 / NATOM)
                + (0.25 * row_facts[start:stop, i:i + 1]) * column_facts[j:j + 1, :]
                for j in range(3)
            ]
            for i in range(3)
        ]

    fill_tile(
        covariance, 128, square, column_facts[3:4, :], count_one[0] - core * 128, count_three[0] - low_place * 128, tile
    )
    ahead_a[...] = tile[aligned(low_place, 64), :]
    ahead_b[...] = tile[aligned(1 - low_place, 64), :]
    tile[...] = tile[...].T
    behind_a[...] = tile[aligned(core, 64), :]
    behind_b[...] = tile[aligned(1 - core, 64), :]


def finish_kernel(got_a, got_b, parts, ahead_a, ahead_b, behind_a, behind_b, behind, ahead):
    core = place_of()[1]

    def ordered(one, two):
        return jnp.where(core == 1, two, one), jnp.where(core == 1, one, two)

    behind[0], behind[2] = ordered(got_a[...], got_b[...])
    behind[1] = jnp.concatenate(ordered(behind_a[...], behind_b[...]), 1)
    ahead[0] = jnp.concatenate([parts[2], parts[3]], 1)
    ahead[1] = jnp.concatenate(ordered(ahead_a[...], ahead_b[...]), 1)
    ahead[2] = jnp.concatenate([parts[0], parts[1]], 1)


def call(kernel, out_shapes, microseconds, scratch=()):
    def run(*args):
        whole = pl.BlockSpec(memory_space=pltpu.VMEM)
        specs = [pl.BlockSpec(memory_space=pltpu.SMEM) if arg.dtype == jnp.int32 else whole for arg in args]
        return pl.pallas_call(
            kernel,
            out_shape=out_shapes,
            in_specs=specs,
            out_specs=jax.tree.map(lambda _: whole, out_shapes),
            scratch_shapes=[pltpu.VMEM(shape, dtype) for shape, dtype in scratch],
            cost_estimate=pl.CostEstimate(flops=0, bytes_accessed=int(microseconds * 3.6e6), transcendentals=0),
            compiler_params=pltpu.CompilerParams(vmem_limit_bytes=VMEM_LIMIT),
        )(*args)

    return run


def f32(*shape):
    return jax.ShapeDtypeStruct(shape, jnp.float32)


def bf16(*shape):
    return jax.ShapeDtypeStruct(shape, jnp.bfloat16)


def shards(coords, frame_count):
    frames = coords.shape[2]
    together = lax.optimization_barrier
    small, wide = jnp.bfloat16, jnp.float32

    own_chip = route(coords, other_chip)
    near_a = route(coords, to_neighbour)
    own_core = route(coords, other_core)
    count_one = route(frame_count, lambda block, rep: (block - 1, rep))
    count_three = route(frame_count, lambda block, rep: (block - 3, rep))

    near_b = route(own_chip, to_neighbour)
    else_a = route(near_a, other_chip)
    own_both = route(own_chip, other_core)
    near_a_core = route(near_a, other_core)
    high, low, square = call(
        prepare_kernel, (bf16(768, DEPTH), bf16(768, DEPTH), f32(frames, 128)), 4.0
    )(coords, own_core, own_chip, own_both)
    sides = [((DEPTH // 2, 384), small), ((DEPTH // 2, 384), small)]
    near_first, facts = call(near_first_kernel, (f32(768, 384), f32(8, 256)), 4.0, sides)(high, low, near_a, near_a_core)
    near_b, else_a, near_first, facts, count_one, count_three = together(
        (near_b, else_a, near_first, facts, count_one, count_three)
    )

    near_b_core = route(near_b, other_core)
    else_a_core = route(else_a, other_core)
    mine, give = call(
        between_kernel,
        (f32(1160, 128), f32(1160, 128)),
        3.0,
        [((384, DEPTH // 2), small), ((384, DEPTH // 2), small), ((DEPTH // 2, 768), small), ((DEPTH // 2, 768), small),
         ((384, 768), wide), ((8, 256), wide), ((8, 256), wide)],
    )(facts, near_b, near_b_core, else_a, else_a_core)
    got = route(give, other_chip)
    near_first, mine = together((near_first, mine))
    near_out_a, near_out_b, parts = call(
        near_kernel,
        (f32(64, frames), f32(64, frames), f32(4, 64, 128)),
        4.0,
        sides + [((768, 384), wide), ((frames, 128), wide), ((128, frames), wide)],
    )(frame_count, count_one, count_three, high, low, square, near_first, facts, near_b, near_b_core)
    got_a = route(near_out_a, lambda b, r: (b + 1, 2 * (r % 2)) if r >= 2 else (b + 3, 2 * (r % 2) + 1))
    got_b = route(near_out_b, lambda b, r: (b + 1, 2 * (r % 2) + 1) if r >= 2 else (b + 3, 2 * (r % 2)))
    parts = lax.all_to_all(parts, "rep", 0, 0)
    got, near_out_a, near_out_b = together((got, near_out_a, near_out_b))

    ahead_a, ahead_b, behind_a, behind_b = call(
        far_kernel,
        (f32(64, 128), f32(64, 128), f32(64, 128), f32(64, 128)),
        1.5,
        [((128, 128), wide), ((128, 128), wide)],
    )(count_one, count_three, mine, got)
    ahead_a = route(ahead_a, lambda block, rep: (block + 1, 2 * (rep % 2) + rep // 2))
    ahead_b = route(ahead_b, lambda block, rep: (block + 1, 2 * (rep % 2) + 1 - rep // 2))
    behind_a = route(behind_a, lambda block, rep: (block + 3, rep))
    behind_b = route(behind_b, lambda block, rep: (block + 3, rep ^ 1))
    return call(finish_kernel, (f32(3, 64, frames), f32(3, 64, frames)), 1.3)(
        got_a, got_b, parts, ahead_a, ahead_b, behind_a, behind_b
    )


def solution(mesh):
    in_specs = (P(None, "rep", "blk"), P("blk"))
    out_specs = (P(None, ("blk", "rep"), None), P(None, ("blk", "rep"), None))
    return jax.shard_map(shards, mesh=mesh, in_specs=in_specs, out_specs=out_specs, check_vma=False)
```

```python
import functools

import jax
import jax.numpy as jnp
from jax import lax
from jax.experimental import pallas as pl
from jax.experimental.pallas import tpu as pltpu
from jax.sharding import PartitionSpec as P

NATOM = 1200
NEWTON = 4
PIECE = 320
DEPTH = 4 * PIECE
VMEM_LIMIT = 12 * 1024 * 1024


def route(array, target):
    blocks, reps = lax.axis_size("blk"), lax.axis_size("rep")
    pairs = []
    for block in range(blocks):
        for rep in range(reps):
            to_block, to_rep = target(block, rep)
            pairs.append((block * reps + rep, (to_block % blocks) * reps + to_rep))
    return lax.ppermute(array, ("blk", "rep"), pairs)


def other_core(block, rep):
    return block, rep ^ 1


def other_chip(block, rep):
    return block, rep ^ 2


def to_neighbour(block, rep):
    return (block - 1, rep + 2) if rep < 2 else (block - 3, rep - 2)


def pair_minor(upper, lower, left, right):
    return upper[left] * lower[right] - upper[right] * lower[left]


def deviation(m, total):
    keyed = [
        [m[0][0] + m[1][1] + m[2][2], m[1][2] - m[2][1], m[2][0] - m[0][2], m[0][1] - m[1][0]],
        [m[1][2] - m[2][1], m[0][0] - m[1][1] - m[2][2], m[0][1] + m[1][0], m[2][0] + m[0][2]],
        [m[2][0] - m[0][2], m[0][1] + m[1][0], -m[0][0] + m[1][1] - m[2][2], m[1][2] + m[2][1]],
        [m[0][1] - m[1][0], m[2][0] + m[0][2], m[1][2] + m[2][1], -m[0][0] - m[1][1] + m[2][2]],
    ]
    top_one, top_two, low_one, low_two = keyed
    det_key = (
        pair_minor(top_one, top_two, 0, 1) * pair_minor(low_one, low_two, 2, 3)
        - pair_minor(top_one, top_two, 0, 2) * pair_minor(low_one, low_two, 1, 3)
        + pair_minor(top_one, top_two, 0, 3) * pair_minor(low_one, low_two, 1, 2)
        + pair_minor(top_one, top_two, 1, 2) * pair_minor(low_one, low_two, 0, 3)
        - pair_minor(top_one, top_two, 1, 3) * pair_minor(low_one, low_two, 0, 2)
        + pair_minor(top_one, top_two, 2, 3) * pair_minor(low_one, low_two, 0, 1)
    )
    det_three = (
        m[0][0] * (m[1][1] * m[2][2] - m[1][2] * m[2][1])
        - m[0][1] * (m[1][0] * m[2][2] - m[1][2] * m[2][0])
        + m[0][2] * (m[1][0] * m[2][1] - m[1][1] * m[2][0])
    )
    square_sum = m[0][0] * m[0][0]
    for first in range(3):
        for second in range(3):
            if first + second > 0:
                square_sum = square_sum + m[first][second] * m[first][second]
    second_coef = -2.0 * square_sum
    first_coef = -8.0 * det_three
    largest = 0.5 * total
    for _ in range(NEWTON):
        squared = largest * largest
        polynomial = squared * squared + second_coef * squared + first_coef * largest + det_key
        derivative = 4.0 * squared * largest + 2.0 * second_coef * largest + first_coef
        largest = largest - polynomial / derivative
    return total - 2.0 * largest


def padded(value):
    return jnp.concatenate([value, jnp.zeros((PIECE - value.shape[0], value.shape[1]), value.dtype)], 0)


def halves(value):
    high = value.astype(jnp.bfloat16)
    return high, (value - high.astype(jnp.float32)).astype(jnp.bfloat16)


def place_of():
    rep = lax.axis_index("rep")
    return rep // 2, rep % 2


def aligned(index, size):
    return pl.ds(pl.multiple_of(index * size, size), size)


def column_sums(pieces):
    return sum(jnp.sum(piece, axis=0, keepdims=True) for piece in pieces)


def products(left_high, left_low, right_high, right_low):
    dot = functools.partial(jnp.dot, preferred_element_type=jnp.float32)
    return dot(left_high, right_high) + dot(left_high, right_low) + dot(left_low, right_high)


def prepare_kernel(a_ref, b_ref, c_ref, d_ref, high_ref, low_ref, square_ref):
    frames = a_ref.shape[2]
    square = jnp.zeros((frames, 1), jnp.float32)
    for comp in range(3):
        pieces = [ref[comp] for ref in (a_ref, b_ref, c_ref, d_ref)]
        centroid = column_sums(pieces) / NATOM
        value = jnp.concatenate([padded(piece - centroid) for piece in pieces], 0).T
        square = square + jnp.sum(value * value, axis=1, keepdims=True)
        high, low = halves(value)
        high_ref[comp * frames:(comp + 1) * frames, :] = high
        low_ref[comp * frames:(comp + 1) * frames, :] = low
    square_ref[...] = jnp.broadcast_to(square / NATOM, square_ref.shape)


def fill_tile(covariance, rows, row_square, column_square, row_limit, column_limit, tile):
    step = 16
    column_valid = lax.broadcasted_iota(jnp.int32, (step, 128), 1) < column_limit
    for at in range(0, rows, step):
        place = lax.broadcasted_iota(jnp.int32, (step, 128), 0) + at
        total = row_square[at:at + step, :] + column_square
        tile[at:at + step, :] = jnp.where(
            (place < row_limit) & column_valid, deviation(covariance(at, at + step), total), 0.0
        )


def right_side(refs, lanes, about, right_high, right_low):
    total, square = [], jnp.zeros((1, 128), jnp.float32)
    for comp in range(3):
        moved = [ref[comp, :, lanes] - about[comp:comp + 1, :] for ref in refs]
        total.append(column_sums(moved))
        square = square + column_sums([value * value for value in moved])
        for place, value in enumerate(moved):
            top, rest = halves(padded(value))
            right_high[place * PIECE:(place + 1) * PIECE, comp * 128:(comp + 1) * 128] = top
            right_low[place * PIECE:(place + 1) * PIECE, comp * 128:(comp + 1) * 128] = rest
    return total, square


def half_facts(refs, out):
    square = 0.0
    for comp in range(3):
        pieces = [ref[comp] for ref in refs]
        mean = column_sums(pieces) / (NATOM / 2)
        square = square + column_sums([(piece - mean) * (piece - mean) for piece in pieces])
        out[comp:comp + 1, :] = mean
    out[3:4, :] = square
    out[4:8, :] = jnp.zeros((4, out.shape[1]), jnp.float32)


def near_first_kernel(high, low, a, b, acc, facts, right_high, right_low):
    half_facts((a, b), facts)
    lanes = aligned(place_of()[1], 128)
    right_side((a, b), lanes, facts[:, lanes], right_high, right_low)
    acc[...] = products(high[:, DEPTH // 2:], low[:, DEPTH // 2:], right_high[...], right_low[...])


def near_kernel(own_count, high, low, square, first, facts, a, b, out, keep, give, own_mask, right_high, right_low, acc, tile):
    low_place, core = place_of()
    lanes = aligned(core, 128)
    about = facts[:, lanes]
    total, column_square = right_side((a, b), lanes, about, right_high, right_low)
    column_square = (column_square + about[3:4, :]) / NATOM
    for comp in range(3):
        offset = total[comp] / NATOM
        column_square = column_square - offset * offset
    acc[...] = first[...] + products(high[:, :DEPTH // 2], low[:, :DEPTH // 2], right_high[...], right_low[...])
    frames = square.shape[0]

    def covariance(start, stop):
        return [
            [acc[i * frames + start:i * frames + stop, j * 128:(j + 1) * 128] * (1.0 / NATOM) for j in range(3)]
            for i in range(3)
        ]

    fill_tile(covariance, frames, square, column_square, own_count[0], 128, tile)
    out[...] = tile[...].T
    keep[...] = tile[aligned(low_place, 128), :]
    give[...] = tile[aligned(1 - low_place, 128), :]
    row = lax.broadcasted_iota(jnp.int32, own_mask.shape, 0) + 64 * lax.axis_index("rep")
    own_mask[...] = jnp.where(row < own_count[0], 1.0, 0.0)


def between_kernel(facts, near_a, near_b, else_a, else_b, mine, give, left_high, left_low, right_high, right_low, acc, here, known):
    low_place, core = place_of()
    half_facts((near_a, near_b), here)
    sign = jnp.where(low_place == 0, 1.0, -1.0)
    square = here[3:4, :] + facts[3:4, :]
    known[...] = jnp.zeros_like(known)
    for comp in range(3):
        apart = here[comp:comp + 1, :] - facts[comp:comp + 1, :]
        known[comp:comp + 1, :] = sign * apart
        square = square + (NATOM / 4) * apart * apart
    known[3:4, :] = square / NATOM
    upper = low_place == 1
    lanes = aligned(core, 128)
    for comp in range(3):
        pieces = [
            jnp.where(upper, one[comp, :, lanes], two[comp, :, lanes]) for one, two in ((near_a, else_a), (near_b, else_b))
        ]
        mean = column_sums(pieces) / (NATOM / 2)
        value = jnp.concatenate([padded(piece - mean) for piece in pieces], 0).T
        high, low = halves(value)
        left_high[comp * 128:(comp + 1) * 128, :] = high
        left_low[comp * 128:(comp + 1) * 128, :] = low
        pieces = [jnp.where(upper, two[comp], one[comp]) for one, two in ((near_a, else_a), (near_b, else_b))]
        mean = column_sums(pieces) / (NATOM / 2)
        for place, piece in enumerate(pieces):
            high, low = halves(padded(piece - mean))
            right_high[place * PIECE:(place + 1) * PIECE, comp * 256:(comp + 1) * 256] = high
            right_low[place * PIECE:(place + 1) * PIECE, comp * 256:(comp + 1) * 256] = low
    acc[...] = products(left_high[...], left_low[...], right_high[...], right_low[...])
    for i in range(3):
        for j in range(3):
            to = pl.ds((3 * i + j) * 128, 128)
            mine[to, :] = acc[i * 128:(i + 1) * 128, aligned(2 * j + low_place, 128)]
            give[to, :] = acc[i * 128:(i + 1) * 128, aligned(2 * j + 1 - low_place, 128)]
    mine[1152:1160, :] = known[:, aligned(jnp.where(upper, core, 0), 128)]
    give[1152:1160, :] = known[:, aligned(jnp.where(upper, core, 1), 128)]


def far_kernel(count_one, count_three, mine, got, tile, turned, other_mask, square):
    low_place, core = place_of()
    one, two = mine[1152:1160, :], got[1152:1160, :]
    row_facts = jnp.where(low_place == 1, one, two).T
    column_facts = jnp.where(low_place == 1, two, one)
    square[...] = jnp.broadcast_to(row_facts[:, 3:4], square.shape)

    def covariance(start, stop):
        return [
            [
                (mine[(3 * i + j) * 128 + start:(3 * i + j) * 128 + stop, :]
                 + got[(3 * i + j) * 128 + start:(3 * i + j) * 128 + stop, :]) * (1.0 / NATOM)
                + (0.25 * row_facts[start:stop, i:i + 1]) * column_facts[j:j + 1, :]
                for j in range(3)
            ]
            for i in range(3)
        ]

    fill_tile(
        covariance, 128, square, column_facts[3:4, :], count_one[0] - core * 128, count_three[0] - low_place * 128, tile
    )
    turned[...] = tile[...].T
    place = lax.broadcasted_iota(jnp.int32, other_mask.shape, 0)
    column = lax.broadcasted_iota(jnp.int32, other_mask.shape, 1)
    other_mask[...] = jnp.where(column < jnp.where(place == 0, count_one[0], count_three[0]), 1.0, 0.0)


def for_core(core, near, keep, got, ahead, behind):
    rows = aligned(core, 64)
    upper = place_of()[0] == 1
    one, two = keep[rows, :], got[rows, :]
    return [near[rows, :], jnp.where(upper, one, two), jnp.where(upper, two, one), ahead[rows, :], behind[rows, :]]


def pack_kernel(near, keep, got, ahead, behind, out):
    out[...] = jnp.concatenate(for_core(1 - place_of()[1], near, keep, got, ahead, behind), 1)


def finish_kernel(own_mask, other_mask, near, keep, got, far_ahead, far_behind, other, behind, ahead):
    core = place_of()[1]
    mine = for_core(core, near, keep, got, far_ahead, far_behind)
    bounds = (0, 256, 384, 512, 640, 768)
    pairs = [(here, other[:, start:stop]) for here, start, stop in zip(mine, bounds, bounds[1:])]
    first = [jnp.where(core == 0, one, two) for one, two in pairs]
    second = [jnp.where(core == 0, two, one) for one, two in pairs]
    valid = own_mask[...] > 0.5
    for at, rows in ((0, first[0]), (2, second[0])):
        behind[at, :, 0:128] = jnp.where(valid, rows[:, 0:128], 0.0)
        behind[at, :, 128:256] = jnp.where(valid, rows[:, 128:256], 0.0)
    for at, place, which in ((0, 1, 0), (2, 2, 1)):
        mask = other_mask[which:which + 1, :] > 0.5
        ahead[at, :, 0:128] = jnp.where(mask[:, 0:128], first[place], 0.0)
        ahead[at, :, 128:256] = jnp.where(mask[:, 128:256], second[place], 0.0)
    for out, place in ((ahead, 3), (behind, 4)):
        out[1, :, 0:128] = first[place]
        out[1, :, 128:256] = second[place]


def call(kernel, out_shapes, microseconds, scratch=()):
    def run(*args):
        whole = pl.BlockSpec(memory_space=pltpu.VMEM)
        specs = [pl.BlockSpec(memory_space=pltpu.SMEM) if arg.dtype == jnp.int32 else whole for arg in args]
        return pl.pallas_call(
            kernel,
            out_shape=out_shapes,
            in_specs=specs,
            out_specs=jax.tree.map(lambda _: whole, out_shapes),
            scratch_shapes=[pltpu.VMEM(shape, dtype) for shape, dtype in scratch],
            cost_estimate=pl.CostEstimate(flops=0, bytes_accessed=int(microseconds * 3.6e6), transcendentals=0),
            compiler_params=pltpu.CompilerParams(vmem_limit_bytes=VMEM_LIMIT),
        )(*args)

    return run


def f32(*shape):
    return jax.ShapeDtypeStruct(shape, jnp.float32)


def bf16(*shape):
    return jax.ShapeDtypeStruct(shape, jnp.bfloat16)


def shards(coords, frame_count):
    frames = coords.shape[2]
    together = lax.optimization_barrier
    small, wide = jnp.bfloat16, jnp.float32

    own_chip = route(coords, other_chip)
    near_a = route(coords, to_neighbour)
    own_core = route(coords, other_core)
    count_one = route(frame_count, lambda block, rep: (block - 1, rep))
    count_three = route(frame_count, lambda block, rep: (block - 3, rep))

    near_b = route(own_chip, to_neighbour)
    else_a = route(near_a, other_chip)
    own_both = route(own_chip, other_core)
    near_a_core = route(near_a, other_core)
    high, low, square = call(
        prepare_kernel, (bf16(768, DEPTH), bf16(768, DEPTH), f32(frames, 128)), 0.3
    )(coords, own_core, own_chip, own_both)
    sides = [((DEPTH // 2, 384), small), ((DEPTH // 2, 384), small)]
    near_first, facts = call(near_first_kernel, (f32(768, 384), f32(8, 256)), 0.3, sides)(high, low, near_a, near_a_core)
    near_b, else_a, high = together((near_b, else_a, high))

    near_b_core = route(near_b, other_core)
    else_a_core = route(else_a, other_core)
    mine, give = call(
        between_kernel,
        (f32(1160, 128), f32(1160, 128)),
        3.0,
        [((384, DEPTH // 2), small), ((384, DEPTH // 2), small), ((DEPTH // 2, 768), small), ((DEPTH // 2, 768), small),
         ((384, 768), wide), ((8, 256), wide), ((8, 256), wide)],
    )(facts, near_b, near_b_core, else_a, else_a_core)
    got = route(give, other_chip)
    near_first, mine = together((near_first, mine))
    near_out, keep, give_chip, own_mask = call(
        near_kernel,
        (f32(128, frames), f32(128, 128), f32(128, 128), f32(64, 128)),
        4.0,
        sides + [((768, 384), wide), ((frames, 128), wide)],
    )(frame_count, high, low, square, near_first, facts, near_b, near_b_core)
    near_got = route(near_out, lambda b, r: (b + 1, 2 * (r % 2)) if r >= 2 else (b + 3, 2 * (r % 2) + 1))
    keep_got = route(give_chip, other_chip)
    got, keep, near_out = together((got, keep, near_out))

    far_ahead, far_behind, other_mask = call(
        far_kernel, (f32(128, 128), f32(128, 128), f32(8, frames)), 1.5, [((128, 128), wide)]
    )(
        count_one, count_three, mine, got
    )
    far_ahead = route(far_ahead, lambda block, rep: (block + 1, 2 * (rep % 2) + rep // 2))
    far_behind = route(far_behind, lambda block, rep: (block + 3, rep))
    held = (near_got, keep, keep_got, far_ahead, far_behind)
    other = route(call(pack_kernel, f32(64, 768), 0.5)(*held), other_core)
    return call(finish_kernel, (f32(3, 64, frames), f32(3, 64, frames)), 1.3)(own_mask, other_mask, *held, other)


def solution(mesh):
    in_specs = (P(None, "rep", "blk"), P("blk"))
    out_specs = (P(None, ("blk", "rep"), None), P(None, ("blk", "rep"), None))
    return jax.shard_map(shards, mesh=mesh, in_specs=in_specs, out_specs=out_specs, check_vma=False)
```

```python
import functools

import jax
import jax.numpy as jnp
from jax import lax
from jax.experimental import pallas as pl
from jax.experimental.pallas import tpu as pltpu
from jax.sharding import PartitionSpec as P

NATOM = 1200
NEWTON = 4
PIECE = 320
DEPTH = 4 * PIECE
VMEM_LIMIT = 12 * 1024 * 1024


def route(array, target):
    blocks, reps = lax.axis_size("blk"), lax.axis_size("rep")
    pairs = []
    for block in range(blocks):
        for rep in range(reps):
            to_block, to_rep = target(block, rep)
            pairs.append((block * reps + rep, (to_block % blocks) * reps + to_rep))
    return lax.ppermute(array, ("blk", "rep"), pairs)


def other_core(block, rep):
    return block, rep ^ 1


def other_chip(block, rep):
    return block, rep ^ 2


def to_neighbour(block, rep):
    return (block - 1, rep + 2) if rep < 2 else (block - 3, rep - 2)


def pair_minor(upper, lower, left, right):
    return upper[left] * lower[right] - upper[right] * lower[left]


def deviation(m, total):
    keyed = [
        [m[0][0] + m[1][1] + m[2][2], m[1][2] - m[2][1], m[2][0] - m[0][2], m[0][1] - m[1][0]],
        [m[1][2] - m[2][1], m[0][0] - m[1][1] - m[2][2], m[0][1] + m[1][0], m[2][0] + m[0][2]],
        [m[2][0] - m[0][2], m[0][1] + m[1][0], -m[0][0] + m[1][1] - m[2][2], m[1][2] + m[2][1]],
        [m[0][1] - m[1][0], m[2][0] + m[0][2], m[1][2] + m[2][1], -m[0][0] - m[1][1] + m[2][2]],
    ]
    top_one, top_two, low_one, low_two = keyed
    det_key = (
        pair_minor(top_one, top_two, 0, 1) * pair_minor(low_one, low_two, 2, 3)
        - pair_minor(top_one, top_two, 0, 2) * pair_minor(low_one, low_two, 1, 3)
        + pair_minor(top_one, top_two, 0, 3) * pair_minor(low_one, low_two, 1, 2)
        + pair_minor(top_one, top_two, 1, 2) * pair_minor(low_one, low_two, 0, 3)
        - pair_minor(top_one, top_two, 1, 3) * pair_minor(low_one, low_two, 0, 2)
        + pair_minor(top_one, top_two, 2, 3) * pair_minor(low_one, low_two, 0, 1)
    )
    det_three = (
        m[0][0] * (m[1][1] * m[2][2] - m[1][2] * m[2][1])
        - m[0][1] * (m[1][0] * m[2][2] - m[1][2] * m[2][0])
        + m[0][2] * (m[1][0] * m[2][1] - m[1][1] * m[2][0])
    )
    square_sum = m[0][0] * m[0][0]
    for first in range(3):
        for second in range(3):
            if first + second > 0:
                square_sum = square_sum + m[first][second] * m[first][second]
    second_coef = -2.0 * square_sum
    first_coef = -8.0 * det_three
    largest = 0.5 * total
    for _ in range(NEWTON):
        squared = largest * largest
        polynomial = squared * squared + second_coef * squared + first_coef * largest + det_key
        derivative = 4.0 * squared * largest + 2.0 * second_coef * largest + first_coef
        largest = largest - polynomial / derivative
    return total - 2.0 * largest


def padded(value):
    return jnp.concatenate([value, jnp.zeros((PIECE - value.shape[0], value.shape[1]), value.dtype)], 0)


def halves(value):
    high = value.astype(jnp.bfloat16)
    return high, (value - high.astype(jnp.float32)).astype(jnp.bfloat16)


def place_of():
    rep = lax.axis_index("rep")
    return rep // 2, rep % 2


def aligned(index, size):
    return pl.ds(pl.multiple_of(index * size, size), size)


def column_sums(pieces):
    return sum(jnp.sum(piece, axis=0, keepdims=True) for piece in pieces)


def products(left_high, left_low, right_high, right_low):
    dot = functools.partial(jnp.dot, preferred_element_type=jnp.float32)
    return dot(left_high, right_high) + dot(left_high, right_low) + dot(left_low, right_high)


def prepare_kernel(a_ref, b_ref, c_ref, d_ref, high_ref, low_ref, square_ref):
    frames = a_ref.shape[2]
    square = jnp.zeros((frames, 1), jnp.float32)
    for comp in range(3):
        pieces = [ref[comp] for ref in (a_ref, b_ref, c_ref, d_ref)]
        centroid = column_sums(pieces) / NATOM
        value = jnp.concatenate([padded(piece - centroid) for piece in pieces], 0).T
        square = square + jnp.sum(value * value, axis=1, keepdims=True)
        high, low = halves(value)
        high_ref[comp * frames:(comp + 1) * frames, :] = high
        low_ref[comp * frames:(comp + 1) * frames, :] = low
    square_ref[...] = jnp.broadcast_to(square / NATOM, square_ref.shape)


def fill_tile(covariance, rows, row_square, column_square, valid, tile):
    step = 16
    column = lax.broadcasted_iota(jnp.int32, (step, 128), 1)
    for at in range(0, rows, step):
        place = lax.broadcasted_iota(jnp.int32, (step, 128), 0) + at
        total = row_square[at:at + step, :] + column_square
        tile[at:at + step, :] = jnp.where(valid(place, column), deviation(covariance(at, at + step), total), 0.0)


def right_side(refs, lanes, about, right_high, right_low):
    total, square = [], jnp.zeros((1, 128), jnp.float32)
    for comp in range(3):
        moved = [ref[comp, :, lanes] - about[comp:comp + 1, :] for ref in refs]
        total.append(column_sums(moved))
        square = square + column_sums([value * value for value in moved])
        for place, value in enumerate(moved):
            top, rest = halves(padded(value))
            right_high[place * PIECE:(place + 1) * PIECE, comp * 128:(comp + 1) * 128] = top
            right_low[place * PIECE:(place + 1) * PIECE, comp * 128:(comp + 1) * 128] = rest
    return total, square


def half_facts(refs, out):
    square = 0.0
    for comp in range(3):
        pieces = [ref[comp] for ref in refs]
        mean = column_sums(pieces) / (NATOM / 2)
        square = square + column_sums([(piece - mean) * (piece - mean) for piece in pieces])
        out[comp:comp + 1, :] = mean
    out[3:4, :] = square
    out[4:8, :] = jnp.zeros((4, out.shape[1]), jnp.float32)


def near_first_kernel(count, high, low, a, b, acc, facts, right_high, right_low):
    half_facts((a, b), facts)
    facts[4:5, :] = jnp.full((1, facts.shape[1]), count[0], jnp.int32).astype(jnp.float32)
    lanes = aligned(place_of()[1], 128)
    right_side((a, b), lanes, facts[:, lanes], right_high, right_low)
    acc[...] = products(high[:, DEPTH // 2:], low[:, DEPTH // 2:], right_high[...], right_low[...])


def near_kernel(own_count, high, low, square, first, facts, a, b, out, keep, give, own_mask, right_high, right_low, acc, tile):
    low_place, core = place_of()
    lanes = aligned(core, 128)
    about = facts[:, lanes]
    total, column_square = right_side((a, b), lanes, about, right_high, right_low)
    column_square = (column_square + about[3:4, :]) / NATOM
    for comp in range(3):
        offset = total[comp] / NATOM
        column_square = column_square - offset * offset
    acc[...] = first[...] + products(high[:, :DEPTH // 2], low[:, :DEPTH // 2], right_high[...], right_low[...])
    frames = square.shape[0]

    def covariance(start, stop):
        return [
            [acc[i * frames + start:i * frames + stop, j * 128:(j + 1) * 128] * (1.0 / NATOM) for j in range(3)]
            for i in range(3)
        ]

    fill_tile(covariance, frames, square, column_square, lambda row, column: row < own_count[0], tile)
    out[...] = tile[...].T
    keep[...] = tile[aligned(low_place, 128), :]
    give[...] = tile[aligned(1 - low_place, 128), :]
    row = lax.broadcasted_iota(jnp.int32, own_mask.shape, 0) + 64 * lax.axis_index("rep")
    own_mask[...] = jnp.where(row < own_count[0], 1.0, 0.0)


def between_kernel(facts, near_a, near_b, else_a, else_b, mine, give, left_high, left_low, right_high, right_low, acc, here, known):
    low_place, core = place_of()
    half_facts((near_a, near_b), here)
    sign = jnp.where(low_place == 0, 1.0, -1.0)
    square = here[3:4, :] + facts[3:4, :]
    known[...] = jnp.zeros_like(known)
    for comp in range(3):
        apart = here[comp:comp + 1, :] - facts[comp:comp + 1, :]
        known[comp:comp + 1, :] = sign * apart
        square = square + (NATOM / 4) * apart * apart
    known[3:4, :] = square / NATOM
    known[4:5, :] = facts[4:5, :]
    upper = low_place == 1
    lanes = aligned(core, 128)
    for comp in range(3):
        pieces = [
            jnp.where(upper, one[comp, :, lanes], two[comp, :, lanes]) for one, two in ((near_a, else_a), (near_b, else_b))
        ]
        mean = column_sums(pieces) / (NATOM / 2)
        value = jnp.concatenate([padded(piece - mean) for piece in pieces], 0).T
        high, low = halves(value)
        left_high[comp * 128:(comp + 1) * 128, :] = high
        left_low[comp * 128:(comp + 1) * 128, :] = low
        pieces = [jnp.where(upper, two[comp], one[comp]) for one, two in ((near_a, else_a), (near_b, else_b))]
        mean = column_sums(pieces) / (NATOM / 2)
        for place, piece in enumerate(pieces):
            high, low = halves(padded(piece - mean))
            right_high[place * PIECE:(place + 1) * PIECE, comp * 256:(comp + 1) * 256] = high
            right_low[place * PIECE:(place + 1) * PIECE, comp * 256:(comp + 1) * 256] = low
    acc[...] = products(left_high[...], left_low[...], right_high[...], right_low[...])
    for i in range(3):
        for j in range(3):
            to = pl.ds((3 * i + j) * 128, 128)
            mine[to, :] = acc[i * 128:(i + 1) * 128, aligned(2 * j + low_place, 128)]
            give[to, :] = acc[i * 128:(i + 1) * 128, aligned(2 * j + 1 - low_place, 128)]
    mine[1152:1160, :] = known[:, aligned(jnp.where(upper, core, 0), 128)]
    give[1152:1160, :] = known[:, aligned(jnp.where(upper, core, 1), 128)]


def far_kernel(mine, got, tile, turned, other_mask, square):
    low_place, core = place_of()
    one, two = mine[1152:1160, :], got[1152:1160, :]
    row_facts = jnp.where(low_place == 1, one, two).T
    column_facts = jnp.where(low_place == 1, two, one)
    square[...] = jnp.broadcast_to(row_facts[:, 3:4], square.shape)

    def covariance(start, stop):
        return [
            [
                (mine[(3 * i + j) * 128 + start:(3 * i + j) * 128 + stop, :]
                 + got[(3 * i + j) * 128 + start:(3 * i + j) * 128 + stop, :]) * (1.0 / NATOM)
                + (0.25 * row_facts[start:stop, i:i + 1]) * column_facts[j:j + 1, :]
                for j in range(3)
            ]
            for i in range(3)
        ]

    count_one = jnp.where(low_place == 1, one, two)[4:5, :]
    count_three = column_facts[4:5, :]

    def valid(row, column):
        row_valid = (row + core * 128).astype(jnp.float32) < count_one
        return row_valid & ((column + low_place * 128).astype(jnp.float32) < count_three)

    fill_tile(covariance, 128, square, column_facts[3:4, :], valid, tile)
    turned[...] = tile[...].T
    for which, count in ((0, count_one), (1, count_three)):
        for half in range(2):
            column = lax.broadcasted_iota(jnp.int32, (1, 128), 1) + half * 128
            other_mask[which:which + 1, half * 128:half * 128 + 128] = jnp.where(
                column.astype(jnp.float32) < count, 1.0, 0.0
            )
    other_mask[2:8, :] = jnp.zeros((6, other_mask.shape[1]), jnp.float32)


def for_core(core, near, keep, got, ahead, behind):
    rows = aligned(core, 64)
    upper = place_of()[0] == 1
    one, two = keep[rows, :], got[rows, :]
    return [near[rows, :], jnp.where(upper, one, two), jnp.where(upper, two, one), ahead[rows, :], behind[rows, :]]


def pack_kernel(near, keep, got, ahead, behind, out):
    out[...] = jnp.concatenate(for_core(1 - place_of()[1], near, keep, got, ahead, behind), 1)


def finish_kernel(own_mask, other_mask, near, keep, got, far_ahead, far_behind, other, behind, ahead):
    core = place_of()[1]
    mine = for_core(core, near, keep, got, far_ahead, far_behind)
    bounds = (0, 256, 384, 512, 640, 768)
    pairs = [(here, other[:, start:stop]) for here, start, stop in zip(mine, bounds, bounds[1:])]
    first = [jnp.where(core == 0, one, two) for one, two in pairs]
    second = [jnp.where(core == 0, two, one) for one, two in pairs]
    valid = own_mask[...] > 0.5
    for at, rows in ((0, first[0]), (2, second[0])):
        behind[at, :, 0:128] = jnp.where(valid, rows[:, 0:128], 0.0)
        behind[at, :, 128:256] = jnp.where(valid, rows[:, 128:256], 0.0)
    for at, place, which in ((0, 1, 0), (2, 2, 1)):
        mask = other_mask[which:which + 1, :] > 0.5
        ahead[at, :, 0:128] = jnp.where(mask[:, 0:128], first[place], 0.0)
        ahead[at, :, 128:256] = jnp.where(mask[:, 128:256], second[place], 0.0)
    for out, place in ((ahead, 3), (behind, 4)):
        out[1, :, 0:128] = first[place]
        out[1, :, 128:256] = second[place]


def call(kernel, out_shapes, microseconds, scratch=()):
    def run(*args):
        whole = pl.BlockSpec(memory_space=pltpu.VMEM)
        specs = [pl.BlockSpec(memory_space=pltpu.SMEM) if arg.dtype == jnp.int32 else whole for arg in args]
        return pl.pallas_call(
            kernel,
            out_shape=out_shapes,
            in_specs=specs,
            out_specs=jax.tree.map(lambda _: whole, out_shapes),
            scratch_shapes=[pltpu.VMEM(shape, dtype) for shape, dtype in scratch],
            cost_estimate=pl.CostEstimate(flops=0, bytes_accessed=int(microseconds * 3.6e6), transcendentals=0),
            compiler_params=pltpu.CompilerParams(vmem_limit_bytes=VMEM_LIMIT),
        )(*args)

    return run


def f32(*shape):
    return jax.ShapeDtypeStruct(shape, jnp.float32)


def bf16(*shape):
    return jax.ShapeDtypeStruct(shape, jnp.bfloat16)


def shards(coords, frame_count):
    frames = coords.shape[2]
    together = lax.optimization_barrier
    small, wide = jnp.bfloat16, jnp.float32

    own_chip = route(coords, other_chip)
    near_a = route(coords, to_neighbour)
    own_core = route(coords, other_core)
    near_count = route(frame_count, to_neighbour)

    near_b = route(own_chip, to_neighbour)
    else_a = route(near_a, other_chip)
    own_both = route(own_chip, other_core)
    near_a_core = route(near_a, other_core)
    high, low, square = call(
        prepare_kernel, (bf16(768, DEPTH), bf16(768, DEPTH), f32(frames, 128)), 0.3
    )(coords, own_core, own_chip, own_both)
    sides = [((DEPTH // 2, 384), small), ((DEPTH // 2, 384), small)]
    near_b, high, near_count = together((near_b, high, near_count))
    near_first, facts = call(near_first_kernel, (f32(768, 384), f32(8, 256)), 0.3, sides)(
        near_count, high, low, near_a, near_a_core
    )
    near_b_core = route(near_b, other_core)
    else_a_core = route(else_a, other_core)
    mine, give = call(
        between_kernel,
        (f32(1160, 128), f32(1160, 128)),
        3.0,
        [((384, DEPTH // 2), small), ((384, DEPTH // 2), small), ((DEPTH // 2, 768), small), ((DEPTH // 2, 768), small),
         ((384, 768), wide), ((8, 256), wide), ((8, 256), wide)],
    )(facts, near_b, near_b_core, else_a, else_a_core)
    got = route(give, other_chip)
    near_first, mine = together((near_first, mine))
    near_out, keep, give_chip, own_mask = call(
        near_kernel,
        (f32(128, frames), f32(128, 128), f32(128, 128), f32(64, 128)),
        4.0,
        sides + [((768, 384), wide), ((frames, 128), wide)],
    )(frame_count, high, low, square, near_first, facts, near_b, near_b_core)
    near_got = route(near_out, lambda b, r: (b + 1, 2 * (r % 2)) if r >= 2 else (b + 3, 2 * (r % 2) + 1))
    keep_got = route(give_chip, other_chip)
    got, keep, near_out = together((got, keep, near_out))

    far_ahead, far_behind, other_mask = call(
        far_kernel, (f32(128, 128), f32(128, 128), f32(8, frames)), 1.5, [((128, 128), wide)]
    )(mine, got)
    far_ahead = route(far_ahead, lambda block, rep: (block + 1, 2 * (rep % 2) + rep // 2))
    far_behind = route(far_behind, lambda block, rep: (block + 3, rep))
    held = (near_got, keep, keep_got, far_ahead, far_behind)
    other = route(call(pack_kernel, f32(64, 768), 0.5)(*held), other_core)
    return call(finish_kernel, (f32(3, 64, frames), f32(3, 64, frames)), 1.3)(own_mask, other_mask, *held, other)


def solution(mesh):
    in_specs = (P(None, "rep", "blk"), P("blk"))
    out_specs = (P(None, ("blk", "rep"), None), P(None, ("blk", "rep"), None))
    return jax.shard_map(shards, mesh=mesh, in_specs=in_specs, out_specs=out_specs, check_vma=False)
```

```python
import functools

import jax
import jax.numpy as jnp
from jax import lax
from jax.experimental import pallas as pl
from jax.experimental.pallas import tpu as pltpu
from jax.sharding import PartitionSpec as P

NATOM = 1200
NEWTON = 4
PIECE = 320
DEPTH = 4 * PIECE
VMEM_LIMIT = 12 * 1024 * 1024


def route(array, target):
    blocks, reps = lax.axis_size("blk"), lax.axis_size("rep")
    pairs = []
    for block in range(blocks):
        for rep in range(reps):
            to_block, to_rep = target(block, rep)
            pairs.append((block * reps + rep, (to_block % blocks) * reps + to_rep))
    return lax.ppermute(array, ("blk", "rep"), pairs)


def other_core(block, rep):
    return block, rep ^ 1


def other_chip(block, rep):
    return block, rep ^ 2


def to_neighbour(block, rep):
    return (block - 1, rep + 2) if rep < 2 else (block - 3, rep - 2)


def pair_minor(upper, lower, left, right):
    return upper[left] * lower[right] - upper[right] * lower[left]


def deviation(m, total):
    keyed = [
        [m[0][0] + m[1][1] + m[2][2], m[1][2] - m[2][1], m[2][0] - m[0][2], m[0][1] - m[1][0]],
        [m[1][2] - m[2][1], m[0][0] - m[1][1] - m[2][2], m[0][1] + m[1][0], m[2][0] + m[0][2]],
        [m[2][0] - m[0][2], m[0][1] + m[1][0], -m[0][0] + m[1][1] - m[2][2], m[1][2] + m[2][1]],
        [m[0][1] - m[1][0], m[2][0] + m[0][2], m[1][2] + m[2][1], -m[0][0] - m[1][1] + m[2][2]],
    ]
    top_one, top_two, low_one, low_two = keyed
    det_key = (
        pair_minor(top_one, top_two, 0, 1) * pair_minor(low_one, low_two, 2, 3)
        - pair_minor(top_one, top_two, 0, 2) * pair_minor(low_one, low_two, 1, 3)
        + pair_minor(top_one, top_two, 0, 3) * pair_minor(low_one, low_two, 1, 2)
        + pair_minor(top_one, top_two, 1, 2) * pair_minor(low_one, low_two, 0, 3)
        - pair_minor(top_one, top_two, 1, 3) * pair_minor(low_one, low_two, 0, 2)
        + pair_minor(top_one, top_two, 2, 3) * pair_minor(low_one, low_two, 0, 1)
    )
    det_three = (
        m[0][0] * (m[1][1] * m[2][2] - m[1][2] * m[2][1])
        - m[0][1] * (m[1][0] * m[2][2] - m[1][2] * m[2][0])
        + m[0][2] * (m[1][0] * m[2][1] - m[1][1] * m[2][0])
    )
    square_sum = m[0][0] * m[0][0]
    for first in range(3):
        for second in range(3):
            if first + second > 0:
                square_sum = square_sum + m[first][second] * m[first][second]
    second_coef = -2.0 * square_sum
    first_coef = -8.0 * det_three
    largest = 0.5 * total
    for _ in range(NEWTON):
        squared = largest * largest
        polynomial = squared * squared + second_coef * squared + first_coef * largest + det_key
        derivative = 4.0 * squared * largest + 2.0 * second_coef * largest + first_coef
        largest = largest - polynomial / derivative
    return total - 2.0 * largest


def padded(value):
    return jnp.concatenate([value, jnp.zeros((PIECE - value.shape[0], value.shape[1]), value.dtype)], 0)


def halves(value):
    high = value.astype(jnp.bfloat16)
    return high, (value - high.astype(jnp.float32)).astype(jnp.bfloat16)


def place_of():
    rep = lax.axis_index("rep")
    return rep // 2, rep % 2


def aligned(index, size):
    return pl.ds(pl.multiple_of(index * size, size), size)


def column_sums(pieces):
    return sum(jnp.sum(piece, axis=0, keepdims=True) for piece in pieces)


def products(left_high, left_low, right_high, right_low):
    dot = functools.partial(jnp.dot, preferred_element_type=jnp.float32)
    return dot(left_high, right_high) + dot(left_high, right_low) + dot(left_low, right_high)


def prepare_kernel(a_ref, b_ref, c_ref, d_ref, high_ref, low_ref, square_ref):
    frames = a_ref.shape[2]
    square = jnp.zeros((frames, 1), jnp.float32)
    for comp in range(3):
        pieces = [ref[comp] for ref in (a_ref, b_ref, c_ref, d_ref)]
        centroid = column_sums(pieces) / NATOM
        value = jnp.concatenate([padded(piece - centroid) for piece in pieces], 0).T
        square = square + jnp.sum(value * value, axis=1, keepdims=True)
        high, low = halves(value)
        high_ref[comp * frames:(comp + 1) * frames, :] = high
        low_ref[comp * frames:(comp + 1) * frames, :] = low
    square_ref[...] = jnp.broadcast_to(square / NATOM, square_ref.shape)


def fill_tile(covariance, rows, row_square, column_square, valid, tile):
    step = 16
    column = lax.broadcasted_iota(jnp.int32, (step, 128), 1)
    for at in range(0, rows, step):
        place = lax.broadcasted_iota(jnp.int32, (step, 128), 0) + at
        total = row_square[at:at + step, :] + column_square
        tile[at:at + step, :] = jnp.where(valid(place, column), deviation(covariance(at, at + step), total), 0.0)


def half_facts(refs, out):
    square = 0.0
    for comp in range(3):
        pieces = [ref[comp] for ref in refs]
        mean = column_sums(pieces) / (NATOM / 2)
        square = square + column_sums([(piece - mean) * (piece - mean) for piece in pieces])
        out[comp:comp + 1, :] = mean
    out[3:4, :] = square
    out[4:8, :] = jnp.zeros((4, out.shape[1]), jnp.float32)


def facts_kernel(count, a, b, facts):
    half_facts((a, b), facts)
    facts[4:5, :] = jnp.full((1, facts.shape[1]), count[0], jnp.int32).astype(jnp.float32)


def near_kernel(own_count, high, low, square, a, b, c, d, out, keep, give, own_mask, right_high, right_low, acc, tile):
    low_place, core = place_of()
    lanes = aligned(core, 128)
    column_square = jnp.zeros((1, 128), jnp.float32)
    for comp in range(3):
        pieces = [ref[comp, :, lanes] for ref in (a, b, c, d)]
        centroid = column_sums(pieces) / NATOM
        for place, piece in enumerate(pieces):
            value = piece - centroid
            column_square = column_square + column_sums([value * value])
            top, rest = halves(padded(value))
            right_high[place * PIECE:(place + 1) * PIECE, comp * 128:(comp + 1) * 128] = top
            right_low[place * PIECE:(place + 1) * PIECE, comp * 128:(comp + 1) * 128] = rest
    column_square = column_square / NATOM
    acc[...] = products(high[...], low[...], right_high[...], right_low[...])
    frames = square.shape[0]

    def covariance(start, stop):
        return [
            [acc[i * frames + start:i * frames + stop, j * 128:(j + 1) * 128] * (1.0 / NATOM) for j in range(3)]
            for i in range(3)
        ]

    fill_tile(covariance, frames, square, column_square, lambda row, column: row < own_count[0], tile)
    out[...] = tile[...].T
    keep[...] = tile[aligned(low_place, 128), :]
    give[...] = tile[aligned(1 - low_place, 128), :]
    row = lax.broadcasted_iota(jnp.int32, own_mask.shape, 0) + 64 * lax.axis_index("rep")
    own_mask[...] = jnp.where(row < own_count[0], 1.0, 0.0)


def between_kernel(facts, near_a, near_b, else_a, else_b, mine, give, left_high, left_low, right_high, right_low, acc, here, known):
    low_place, core = place_of()
    half_facts((near_a, near_b), here)
    sign = jnp.where(low_place == 0, 1.0, -1.0)
    square = here[3:4, :] + facts[3:4, :]
    known[...] = jnp.zeros_like(known)
    for comp in range(3):
        apart = here[comp:comp + 1, :] - facts[comp:comp + 1, :]
        known[comp:comp + 1, :] = sign * apart
        square = square + (NATOM / 4) * apart * apart
    known[3:4, :] = square / NATOM
    known[4:5, :] = facts[4:5, :]
    upper = low_place == 1
    lanes = aligned(core, 128)
    for comp in range(3):
        pieces = [
            jnp.where(upper, one[comp, :, lanes], two[comp, :, lanes]) for one, two in ((near_a, else_a), (near_b, else_b))
        ]
        mean = column_sums(pieces) / (NATOM / 2)
        value = jnp.concatenate([padded(piece - mean) for piece in pieces], 0).T
        high, low = halves(value)
        left_high[comp * 128:(comp + 1) * 128, :] = high
        left_low[comp * 128:(comp + 1) * 128, :] = low
        pieces = [jnp.where(upper, two[comp], one[comp]) for one, two in ((near_a, else_a), (near_b, else_b))]
        mean = column_sums(pieces) / (NATOM / 2)
        for place, piece in enumerate(pieces):
            high, low = halves(padded(piece - mean))
            right_high[place * PIECE:(place + 1) * PIECE, comp * 256:(comp + 1) * 256] = high
            right_low[place * PIECE:(place + 1) * PIECE, comp * 256:(comp + 1) * 256] = low
    acc[...] = products(left_high[...], left_low[...], right_high[...], right_low[...])
    for i in range(3):
        for j in range(3):
            to = pl.ds((3 * i + j) * 128, 128)
            mine[to, :] = acc[i * 128:(i + 1) * 128, aligned(2 * j + low_place, 128)]
            give[to, :] = acc[i * 128:(i + 1) * 128, aligned(2 * j + 1 - low_place, 128)]
    mine[1152:1160, :] = known[:, aligned(jnp.where(upper, core, 0), 128)]
    give[1152:1160, :] = known[:, aligned(jnp.where(upper, core, 1), 128)]


def far_kernel(mine, got, tile, turned, other_mask, square):
    low_place, core = place_of()
    one, two = mine[1152:1160, :], got[1152:1160, :]
    row_facts = jnp.where(low_place == 1, one, two).T
    column_facts = jnp.where(low_place == 1, two, one)
    square[...] = jnp.broadcast_to(row_facts[:, 3:4], square.shape)

    def covariance(start, stop):
        return [
            [
                (mine[(3 * i + j) * 128 + start:(3 * i + j) * 128 + stop, :]
                 + got[(3 * i + j) * 128 + start:(3 * i + j) * 128 + stop, :]) * (1.0 / NATOM)
                + (0.25 * row_facts[start:stop, i:i + 1]) * column_facts[j:j + 1, :]
                for j in range(3)
            ]
            for i in range(3)
        ]

    count_one = jnp.where(low_place == 1, one, two)[4:5, :]
    count_three = column_facts[4:5, :]

    def valid(row, column):
        row_valid = (row + core * 128).astype(jnp.float32) < count_one
        return row_valid & ((column + low_place * 128).astype(jnp.float32) < count_three)

    fill_tile(covariance, 128, square, column_facts[3:4, :], valid, tile)
    turned[...] = tile[...].T
    for which, count in ((0, count_one), (1, count_three)):
        for half in range(2):
            column = lax.broadcasted_iota(jnp.int32, (1, 128), 1) + half * 128
            other_mask[which:which + 1, half * 128:half * 128 + 128] = jnp.where(
                column.astype(jnp.float32) < count, 1.0, 0.0
            )
    other_mask[2:8, :] = jnp.zeros((6, other_mask.shape[1]), jnp.float32)


def for_core(core, near, keep, got, ahead, behind):
    rows = aligned(core, 64)
    upper = place_of()[0] == 1
    one, two = keep[rows, :], got[rows, :]
    return [near[rows, :], jnp.where(upper, one, two), jnp.where(upper, two, one), ahead[rows, :], behind[rows, :]]


def pack_kernel(near, keep, got, ahead, behind, out):
    out[...] = jnp.concatenate(for_core(1 - place_of()[1], near, keep, got, ahead, behind), 1)


def finish_kernel(own_mask, other_mask, near, keep, got, far_ahead, far_behind, other, behind, ahead):
    core = place_of()[1]
    mine = for_core(core, near, keep, got, far_ahead, far_behind)
    bounds = (0, 256, 384, 512, 640, 768)
    pairs = [(here, other[:, start:stop]) for here, start, stop in zip(mine, bounds, bounds[1:])]
    first = [jnp.where(core == 0, one, two) for one, two in pairs]
    second = [jnp.where(core == 0, two, one) for one, two in pairs]
    valid = own_mask[...] > 0.5
    for at, rows in ((0, first[0]), (2, second[0])):
        behind[at, :, 0:128] = jnp.where(valid, rows[:, 0:128], 0.0)
        behind[at, :, 128:256] = jnp.where(valid, rows[:, 128:256], 0.0)
    for at, place, which in ((0, 1, 0), (2, 2, 1)):
        mask = other_mask[which:which + 1, :] > 0.5
        ahead[at, :, 0:128] = jnp.where(mask[:, 0:128], first[place], 0.0)
        ahead[at, :, 128:256] = jnp.where(mask[:, 128:256], second[place], 0.0)
    for out, place in ((ahead, 3), (behind, 4)):
        out[1, :, 0:128] = first[place]
        out[1, :, 128:256] = second[place]


def call(kernel, out_shapes, microseconds, scratch=()):
    def run(*args):
        whole = pl.BlockSpec(memory_space=pltpu.VMEM)
        specs = [pl.BlockSpec(memory_space=pltpu.SMEM) if arg.dtype == jnp.int32 else whole for arg in args]
        return pl.pallas_call(
            kernel,
            out_shape=out_shapes,
            in_specs=specs,
            out_specs=jax.tree.map(lambda _: whole, out_shapes),
            scratch_shapes=[pltpu.VMEM(shape, dtype) for shape, dtype in scratch],
            cost_estimate=pl.CostEstimate(flops=0, bytes_accessed=int(microseconds * 3.6e6), transcendentals=0),
            compiler_params=pltpu.CompilerParams(vmem_limit_bytes=VMEM_LIMIT),
        )(*args)

    return run


def f32(*shape):
    return jax.ShapeDtypeStruct(shape, jnp.float32)


def bf16(*shape):
    return jax.ShapeDtypeStruct(shape, jnp.bfloat16)


def shards(coords, frame_count):
    frames = coords.shape[2]
    together = lax.optimization_barrier
    small, wide = jnp.bfloat16, jnp.float32

    own_chip = route(coords, other_chip)
    near_a = route(coords, to_neighbour)
    own_core = route(coords, other_core)
    near_count = route(frame_count, to_neighbour)

    near_b = route(own_chip, to_neighbour)
    else_a = route(near_a, other_chip)
    own_both = route(own_chip, other_core)
    near_a_core = route(near_a, other_core)
    high, low, square = call(
        prepare_kernel, (bf16(768, DEPTH), bf16(768, DEPTH), f32(frames, 128)), 0.3
    )(coords, own_core, own_chip, own_both)
    near_b, high, near_count = together((near_b, high, near_count))
    facts = call(facts_kernel, f32(8, 256), 0.3)(near_count, near_a, near_a_core)
    near_b_core = route(near_b, other_core)
    else_a_core = route(else_a, other_core)
    mine, give = call(
        between_kernel,
        (f32(1160, 128), f32(1160, 128)),
        3.0,
        [((384, DEPTH // 2), small), ((384, DEPTH // 2), small), ((DEPTH // 2, 768), small), ((DEPTH // 2, 768), small),
         ((384, 768), wide), ((8, 256), wide), ((8, 256), wide)],
    )(facts, near_b, near_b_core, else_a, else_a_core)
    got = route(give, other_chip)
    high, mine = together((high, mine))
    near_out, keep, give_chip, own_mask = call(
        near_kernel,
        (f32(128, frames), f32(128, 128), f32(128, 128), f32(64, 128)),
        4.0,
        [((DEPTH, 384), small), ((DEPTH, 384), small), ((768, 384), wide), ((frames, 128), wide)],
    )(frame_count, high, low, square, near_b, near_b_core, near_a, near_a_core)
    near_got = route(near_out, lambda b, r: (b + 1, 2 * (r % 2)) if r >= 2 else (b + 3, 2 * (r % 2) + 1))
    keep_got = route(give_chip, other_chip)
    got, keep, near_out = together((got, keep, near_out))

    far_ahead, far_behind, other_mask = call(
        far_kernel, (f32(128, 128), f32(128, 128), f32(8, frames)), 1.5, [((128, 128), wide)]
    )(mine, got)
    far_ahead = route(far_ahead, lambda block, rep: (block + 1, 2 * (rep % 2) + rep // 2))
    far_behind = route(far_behind, lambda block, rep: (block + 3, rep))
    held = (near_got, keep, keep_got, far_ahead, far_behind)
    other = route(call(pack_kernel, f32(64, 768), 0.5)(*held), other_core)
    return call(finish_kernel, (f32(3, 64, frames), f32(3, 64, frames)), 1.3)(own_mask, other_mask, *held, other)


def solution(mesh):
    in_specs = (P(None, "rep", "blk"), P("blk"))
    out_specs = (P(None, ("blk", "rep"), None), P(None, ("blk", "rep"), None))
    return jax.shard_map(shards, mesh=mesh, in_specs=in_specs, out_specs=out_specs, check_vma=False)
```
